512 devices in a mesh: graph: 16 (over z, core), config: 32 (over y, x).
Axes of the slice: x: 4, y: 8, z: 8, core: 2. Of those that a mesh axis runs over, the one named last changes fastest.
Arguments:
- features: bfloat16 [64, 8192, 128], P('config', 'graph'), may hold values from -6 to 6
- cotangent: bfloat16 [64, 8192, 128], P(None, ('graph', 'config')), may hold values from -6 to 6
- sage_weight: bfloat16 [2, 128, 128], replicated, may hold values from -0.5 to 0.5
- attn_weight: bfloat16 [4, 128, 128], replicated, may hold values from -0.5 to 0.5
- tile_vals: bfloat16 [192, 128, 128], P('graph'), may hold values from -0.375 to 0.375
- tile_dst: int32 [192], P('graph'), may hold values from 0 to 3
- tile_src: int32 [192], P('graph'), may hold values from 0 to 3
- tile_count: int32 [16], P('graph'), may hold values from 3 to 12, as said below
- hub_ids: int32 [128], P('graph'), may hold values from 0 to 8191, as said below
- hub_weight: bfloat16 [8192, 128], P('graph'), may hold values from -0.5 to 0.5
Outputs:
- layer_out: bfloat16 [64, 8192, 128], P(None, ('graph', 'config'))
- grad_features: bfloat16 [64, 8192, 128], P('config', 'graph')
- grad_weights: float32 [16, 6, 128, 128], P('graph')
The draws below stay inside these ranges and needn't reach their ends.
Inputs may be any that keep to these rules, and one draw needn't show every extreme that they name: Slot t of slab g (t counted within the slab) is live when t < tile_count[g]; some slab has all 12 slots live. `hub_ids`: entries g * 8 to (g+1) * 8 - 1 are distinct nodes of slab g.
All inputs are finite; a program needn't handle non-finite values.
Results may differ from the reference program's by a relative error of at most 0.024.
Values may be sent and summed in bfloat16 or wider, within the bound.
A program may use at most 64 MiB of HBM per device.

```python
import math
import jax
import jax.numpy as jnp
from jax import lax

F = 128
HEADS = 4
TILE = 128
NODE_DEV = 512
HUB_DEV = 8
TILES_DEV = 12
NODES = 8192
LAYOUTS = 64
TILES = 192
HUB = 128
SHARE = 16
N_GRAPH = 16
N_CONFIG = 32


def draw_tile_count(key, part):
    first_key, second_key = jax.random.split(key)
    counts = jax.random.randint(first_key, (N_GRAPH,), TILES_DEV // 4, TILES_DEV + 1)
    busiest = jax.random.randint(second_key, (), 0, N_GRAPH)
    filled = jnp.where(jnp.arange(N_GRAPH) == busiest, TILES_DEV, counts)
    return filled.astype(jnp.int32)


def draw_hub_ids(key, part):
    slab_keys = jax.random.split(key, N_GRAPH)
    picks = jax.vmap(lambda slab_key: jax.random.permutation(slab_key, NODE_DEV)[:HUB_DEV])(slab_keys)
    offsets = jnp.arange(N_GRAPH, dtype=jnp.int32)[:, None] * NODE_DEV
    return (picks.astype(jnp.int32) + offsets).reshape(-1).astype(jnp.int32)


def with_ends(entries, own_key, least, largest):
    longest = entries.shape.index(max(entries.shape))
    spots = []
    for shift in (0, 1):
        where = [jax.random.randint(jax.random.fold_in(own_key, axis), (), 0, length) for axis, length in enumerate(entries.shape)]
        where[longest] = (where[longest] + shift) % entries.shape[longest]
        spots.append(tuple(where))
    return entries.at[spots[0]].set(least).at[spots[1]].set(largest)


def level_of(stream_key, dims, cuts, least, largest):
    def one(dim, shards_of):
        heights = jax.random.uniform(jax.random.fold_in(jax.random.fold_in(stream_key, 6), dim), (shards_of,), jnp.float32, least / len(cuts), largest / len(cuts))
        return jnp.repeat(jnp.exp(heights), dims[dim] // shards_of).reshape((-1,) + (1,) * (len(dims) - dim - 1))

    gain = one(*cuts[0])
    for cut in cuts[1:]:
        gain = gain * one(*cut)
    return gain


def normal_values(own_key, dims, deviation, bound, cuts=(), kind=jnp.bfloat16):
    gain = level_of(own_key, dims, cuts, -0.22, 0.18) if cuts else 1.0
    drawn = jax.random.normal(own_key, dims, jnp.float32) * deviation * gain
    return jnp.minimum(jnp.maximum(drawn, -bound), bound).astype(kind)


def setup_inputs(seed: int = 0) -> dict:
    key_of = jax.random.split(jax.random.key(seed), 11)
    return {
        "features": normal_values(key_of[0], (LAYOUTS, NODES, F), 1.0, 6.0, ((0, 32), (1, 16))),
        "cotangent": normal_values(key_of[1], (LAYOUTS, NODES, F), 1.0, 6.0, ((1, 512),)),
        "sage_weight": normal_values(key_of[2], (2, F, F), F ** -0.5, 0.5),
        "attn_weight": normal_values(key_of[3], (4, F, F), F ** -0.5, 0.5),
        "tile_vals": normal_values(key_of[4], (TILES, TILE, TILE), (2 * TILE) ** -0.5, 0.375, ((0, 16),)),
        "tile_dst": with_ends(jax.random.randint(key_of[5], (TILES,), 0, NODE_DEV // TILE), jax.random.fold_in(key_of[5], 1), 0, (NODE_DEV // TILE) - 1).astype(jnp.int32),
        "tile_src": with_ends(jax.random.randint(key_of[6], (TILES,), 0, NODE_DEV // TILE), jax.random.fold_in(key_of[6], 1), 0, (NODE_DEV // TILE) - 1).astype(jnp.int32),
        "tile_count": draw_tile_count(jax.random.fold_in(key_of[10], 71), 0),
        "hub_ids": draw_hub_ids(jax.random.fold_in(key_of[10], 71), 0),
        "hub_weight": normal_values(key_of[9], (NODES, HUB), HUB ** -0.5, 0.5, ((0, 16),)),
    }


CAP = 20.0

def attend(queries, key_rows, value_rows):
    layout_count, node_count, feature_width = queries.shape
    head_size = feature_width // HEADS
    split = (layout_count, node_count, HEADS, head_size)
    query_b = queries.reshape(split)
    key_b = key_rows.reshape(split)
    value_b = value_rows.reshape(split)
    scores = jnp.einsum('lkhd,mkhd->khlm', query_b, key_b, preferred_element_type=jnp.float32) / math.sqrt(head_size)
    capped = CAP * jnp.tanh(scores / CAP)
    weights = jnp.exp(capped)
    attention = weights / lax.optimization_barrier(jnp.sum(weights, axis=-1, keepdims=True))
    attention = attention.astype(value_b.dtype)
    mixture = jnp.einsum('khlm,mkhd->lkhd', attention, value_b, preferred_element_type=jnp.float32)
    return mixture.reshape(layout_count, node_count, feature_width).astype(queries.dtype)

def project(flat_rows, weight):
    return jnp.dot(flat_rows, weight, preferred_element_type=jnp.float32)

def project_back(flat_rows, weight):
    return jnp.dot(flat_rows, weight.T, preferred_element_type=jnp.float32)

def outer_sum(left_rows, right_rows):
    return jnp.dot(left_rows.T, right_rows, preferred_element_type=jnp.float32)

def sage_forward(feats, aggregate, sage_weight):
    shaped = feats.shape
    width_f = shaped[-1]
    pre_acts = project(feats.reshape(-1, width_f), sage_weight[0]) + project(aggregate.reshape(-1, width_f), sage_weight[1])
    hidden = jax.nn.silu(pre_acts).astype(jnp.bfloat16)
    return (pre_acts.reshape(shaped), hidden.reshape(shaped))

def node_forward(hidden, attn_weight):
    shaped = hidden.shape
    width_f = shaped[-1]
    three = (shaped[0], -1, width_f)
    flat_hidden = hidden.reshape(-1, width_f)
    queries = project(flat_hidden, attn_weight[0]).astype(jnp.bfloat16)
    key_rows = project(flat_hidden, attn_weight[1]).astype(jnp.bfloat16)
    value_rows = project(flat_hidden, attn_weight[2]).astype(jnp.bfloat16)
    mixture = attend(queries.reshape(three), key_rows.reshape(three), value_rows.reshape(three))
    output = (flat_hidden.astype(jnp.float32) + project(mixture.reshape(-1, width_f), attn_weight[3])).astype(jnp.bfloat16)
    return (output.reshape(shaped), queries.reshape(shaped), key_rows.reshape(shaped), value_rows.reshape(shaped), mixture.reshape(shaped))

def node_backward(cot_rows, hidden, queries, key_rows, value_rows, mixture, attn_weight):
    shaped = hidden.shape
    width_f = shaped[-1]
    three = (shaped[0], -1, width_f)
    flat_cot = cot_rows.reshape(-1, width_f)
    grad_mix = project_back(flat_cot, attn_weight[3]).astype(jnp.bfloat16)
    grad_wo = outer_sum(mixture.reshape(-1, width_f), flat_cot)
    unused, pullback = jax.vjp(attend, queries.reshape(three), key_rows.reshape(three), value_rows.reshape(three))
    grad_q, grad_k, grad_v = pullback(grad_mix.reshape(three))
    flat_q = grad_q.reshape(-1, width_f)
    flat_k = grad_k.reshape(-1, width_f)
    flat_v = grad_v.reshape(-1, width_f)
    grad_hidden = (flat_cot.astype(jnp.float32) + project_back(flat_q, attn_weight[0]) + project_back(flat_k, attn_weight[1]) + project_back(flat_v, attn_weight[2])).astype(jnp.bfloat16)
    flat_hidden = hidden.reshape(-1, width_f)
    grads = jnp.stack([outer_sum(flat_hidden, flat_q), outer_sum(flat_hidden, flat_k), outer_sum(flat_hidden, flat_v), grad_wo])
    return (grad_hidden.reshape(shaped), grads)

def sage_backward(grad_hidden, pre_acts, feats, aggregate, sage_weight):
    shaped = feats.shape
    width_f = shaped[-1]
    flat_pre = pre_acts.reshape(-1, width_f)
    sigmoid_pre = jax.nn.sigmoid(flat_pre)
    grad_pre = (grad_hidden.reshape(-1, width_f).astype(jnp.float32) * sigmoid_pre * (1.0 + flat_pre * (1.0 - sigmoid_pre))).astype(jnp.bfloat16)
    grads = jnp.stack([outer_sum(feats.reshape(-1, width_f), grad_pre), outer_sum(aggregate.reshape(-1, width_f), grad_pre)])
    grad_self = project_back(grad_pre, sage_weight[0]).astype(jnp.bfloat16).reshape(shaped)
    grad_agg = project_back(grad_pre, sage_weight[1]).astype(jnp.bfloat16).reshape(shaped)
    return (grad_self, grad_agg, grads)

def reference(features, cotangent, sage_weight, attn_weight, tile_vals, tile_dst, tile_src, tile_count, hub_ids, hub_weight):
    slab_count = N_GRAPH
    span_count = N_GRAPH * N_CONFIG
    hub_rows = features[:, hub_ids]
    by_slab = features.reshape(LAYOUTS, slab_count, NODE_DEV, F).transpose(1, 0, 2, 3)
    tiles_slab = tile_vals.reshape(slab_count, TILES_DEV, TILE, TILE)
    dst_slab = tile_dst.reshape(slab_count, TILES_DEV)
    src_slab = tile_src.reshape(slab_count, TILES_DEV)
    hubw_slab = hub_weight.reshape(slab_count, NODE_DEV, HUB)
    block_ids = jnp.arange(NODE_DEV // TILE, dtype=jnp.int32)[:, None]

    def placement(targets, count):
        live = (jnp.arange(TILES_DEV, dtype=jnp.int32) < count).astype(jnp.float32)
        return (targets[None, :] == block_ids).astype(jnp.float32) * live[None, :]

    def forward_slab(packed):
        feats, tiles, dst, src, count, hubw = packed
        gathered = feats.reshape(LAYOUTS, -1, TILE, F)[:, src]
        products = jnp.einsum('tij,ltjf->ltif', tiles.astype(jnp.float32), gathered.astype(jnp.float32), precision=lax.Precision.HIGHEST)
        tile_sum = jnp.einsum('bt,ltif->lbif', placement(dst, count), products, precision=lax.Precision.HIGHEST).reshape(LAYOUTS, NODE_DEV, F)
        hub_sum = jnp.einsum('nj,ljf->lnf', hubw.astype(jnp.float32), hub_rows.astype(jnp.float32), precision=lax.Precision.HIGHEST)
        aggregate = (tile_sum + hub_sum).astype(jnp.bfloat16)
        pre_acts, hidden = sage_forward(feats, aggregate, sage_weight)
        return (aggregate, hidden)
    aggregates, hiddens = lax.map(forward_slab, (by_slab, tiles_slab, dst_slab, src_slab, tile_count, hubw_slab))
    hidden_all = hiddens.transpose(1, 0, 2, 3).reshape(LAYOUTS, span_count, SHARE, F).transpose(1, 0, 2, 3)
    cot_all = cotangent.reshape(LAYOUTS, span_count, SHARE, F).transpose(1, 0, 2, 3)

    def node_span(packed):
        hidden, cot_rows = packed
        output, queries, key_rows, value_rows, mixture = node_forward(hidden, attn_weight)
        grad_hidden, grads = node_backward(cot_rows, hidden, queries, key_rows, value_rows, mixture, attn_weight)
        return (output, grad_hidden, grads)
    outputs, grad_hiddens, attn_parts = lax.map(node_span, (hidden_all, cot_all))
    layer_out = outputs.transpose(1, 0, 2, 3).reshape(LAYOUTS, NODES, F)
    grad_slab = grad_hiddens.transpose(1, 0, 2, 3).reshape(LAYOUTS, slab_count, NODE_DEV, F).transpose(1, 0, 2, 3)

    def backward_slab(packed):
        feats, aggregate, grad_hidden, hubw = packed
        pre_acts, unused = sage_forward(feats, aggregate, sage_weight)
        grad_self, grad_agg, grads = sage_backward(grad_hidden, pre_acts, feats, aggregate, sage_weight)
        hub_part = jnp.einsum('nj,lnf->ljf', hubw.astype(jnp.float32), grad_agg.astype(jnp.float32), precision=lax.Precision.HIGHEST)
        return (grad_self, grad_agg, grads, hub_part)
    grad_selfs, grad_aggs, sage_parts, hub_parts = lax.map(backward_slab, (by_slab, aggregates, grad_slab, hubw_slab))
    hub_total = lax.optimization_barrier(jnp.sum(hub_parts, axis=0))

    def finish_slab(packed):
        index, grad_self, grad_agg, tiles, dst, src, count = packed
        gathered = grad_agg.reshape(LAYOUTS, -1, TILE, F)[:, dst]
        products = jnp.einsum('tij,ltif->ltjf', tiles.astype(jnp.float32), gathered.astype(jnp.float32), precision=lax.Precision.HIGHEST)
        back_rows = jnp.einsum('bt,ltjf->lbjf', placement(src, count), products, precision=lax.Precision.HIGHEST).reshape(LAYOUTS, NODE_DEV, F)
        local_ids = lax.dynamic_slice_in_dim(hub_ids, (index * HUB_DEV).astype(jnp.int32), HUB_DEV) - (index * NODE_DEV).astype(jnp.int32)
        hub_piece = lax.dynamic_slice_in_dim(hub_total, (index * HUB_DEV).astype(jnp.int32), HUB_DEV, 1)
        totals = grad_self.astype(jnp.float32) + back_rows
        totals = totals.at[:, local_ids].add(hub_piece)
        return totals.astype(jnp.bfloat16)
    slab_ids = jnp.arange(slab_count, dtype=jnp.int32)
    grads_x = lax.map(finish_slab, (slab_ids, grad_selfs, grad_aggs, tiles_slab, dst_slab, src_slab, tile_count))
    grad_features = grads_x.transpose(1, 0, 2, 3).reshape(LAYOUTS, NODES, F)
    attn_slab = lax.optimization_barrier(jnp.sum(attn_parts.reshape(slab_count, N_CONFIG, 4, F, F), axis=1))
    grad_weights = jnp.concatenate([sage_parts, attn_slab], axis=1)
    grad_weights = grad_weights / math.sqrt(LAYOUTS * NODE_DEV)
    return (layer_out, grad_features, grad_weights)
```

```python
import functools
import math

import jax
import jax.numpy as jnp
from jax import lax
from jax.experimental import pallas as pl
from jax.experimental.pallas import tpu as pltpu
from jax.sharding import PartitionSpec as P

HEADS = 4
CAP = 20.0
F = 128
MESH = pl.DeviceIdType.MESH
BF = jnp.bfloat16
F32 = jnp.float32


def mm(a, b):
    return jnp.dot(a, b, preferred_element_type=F32)


def mm_nt(a, b):
    return lax.dot_general(a, b, (((1,), (1,)), ((), ())), preferred_element_type=F32)


def mm_tn(a, b):
    return lax.dot_general(a, b, (((0,), (0,)), ((), ())), preferred_element_type=F32)


def kernel(
    feat, cot, sw, aw, tiles, dst, src, cnt, ids, hubw,
    lo_out, gf_out, gw_out,
    adj, adj_t, hub_t, fa_t, acc32, dsil, agg, hid, hall, h32, c32, g32, o32,
    dqkv, hn, mixn, cotn, gmn, gsend, gback, gpre, gacat, tot32,
    hubloc, hub_all, hg_src, hg_buf, ars_src, ars_buf, aag_src, aag_buf,
    srs_src, srs_buf, sag_src, sag_buf,
    fwd_s, fwd_r, back_s, back_r, hub_s, hub_r, hg_s, hg_r,
    ars_s, ars_r, aag_s, aag_r, srs_s, srs_r, sag_s, sag_r,
):
    g = lax.axis_index("graph")
    c = lax.axis_index("config")
    n_g = lax.axis_size("graph")
    n_c = lax.axis_size("config")
    barrier = pltpu.get_barrier_semaphore()

    def hello_config(k, carry):
        pl.semaphore_signal(barrier, inc=1, device_id={"config": lax.rem(c + k, n_c)}, device_id_type=MESH)
        return carry

    def hello_graph(k, carry):
        pl.semaphore_signal(barrier, inc=1, device_id={"graph": lax.rem(g + k, n_g)}, device_id_type=MESH)
        return carry

    lax.fori_loop(1, n_g, hello_graph, 0)
    lax.fori_loop(1, n_c, hello_config, 0)

    def send(src_ref, dst_ref, send_sem, recv_sem, where):
        pltpu.make_async_remote_copy(
            src_ref=src_ref, dst_ref=dst_ref, send_sem=send_sem, recv_sem=recv_sem,
            device_id=where, device_id_type=MESH,
        ).start()

    def wait_bytes(ref, sem):
        pltpu.make_async_copy(ref, ref, sem).wait()

    base = g * 512
    row = lax.broadcasted_iota(jnp.int32, (16, 512), 0)
    col = lax.broadcasted_iota(jnp.int32, (16, 512), 1)
    want = jnp.full((16, 512), -1, jnp.int32)
    for j in range(8):
        want = jnp.where(row == j, ids[j] - base, want)
    onehot = jnp.where(col == want, 1.0, 0.0).astype(BF)
    x_cat = jnp.concatenate([feat[0], feat[1]], axis=1)
    rows_hub = mm(onehot, x_cat)
    hubloc[...] = jnp.concatenate([rows_hub[:8, :F], rows_hub[:8, F:]], axis=0).astype(BF)

    pl.semaphore_wait(barrier, n_g + n_c - 2)

    pltpu.make_async_copy(hubloc, hub_all.at[g], hub_r).start()

    def send_hub(k, carry):
        send(hubloc, hub_all.at[g], hub_s, hub_r, {"graph": lax.rem(g + k, n_g)})
        return carry

    lax.fori_loop(1, n_g, send_hub, 0)

    def build(b, carry):
        at = pl.multiple_of(b * 128, 128)
        for s in range(4):
            acc = jnp.zeros((128, 128), F32)
            for t in range(12):
                live = (dst[t] == b) & (src[t] == s) & (t < cnt[0])
                acc = acc + jnp.where(live, 1.0, 0.0) * tiles[t].astype(F32)
            adj[pl.ds(at, 128), s * 128 : (s + 1) * 128] = acc.astype(BF)
            adj_t[s * 128 : (s + 1) * 128, pl.ds(at, 128)] = acc.T.astype(BF)
        return carry

    lax.fori_loop(0, 4, build, 0)

    def first(b, carry):
        rows = pl.ds(pl.multiple_of(b * 128, 128), 128)
        acc32[rows, :] = mm(adj[rows, :], jnp.concatenate([feat[0], feat[1]], axis=1))
        return carry

    lax.fori_loop(0, 4, first, 0)

    wait_bytes(hub_all, hub_r)
    hubs = hub_all[...].astype(F32).reshape(16, 2, 8, F)
    hub_cat = jnp.concatenate(
        [hubs[:, 0].reshape(128, F).astype(BF), hubs[:, 1].reshape(128, F).astype(BF)], axis=1
    )
    w_sage = sw[...].reshape(2 * F, F)

    def forward(i, carry):
        b = lax.rem(c // 8 + i, 4)
        rows = pl.ds(pl.multiple_of(b * 128, 128), 128)
        acc = acc32[rows, :] + mm(hubw[rows, :], hub_cat)
        for l in range(2):
            a_l = acc[:, l * F : (l + 1) * F].astype(BF)
            agg[l, rows, :] = a_l
            pre = mm(jnp.concatenate([feat[l, rows, :], a_l], axis=1), w_sage)
            sig = 1.0 / (1.0 + jnp.exp(-pre))
            dsil[l, rows, :] = sig * (1.0 + pre * (1.0 - sig))
            hid[l, rows, :] = (pre * sig).astype(BF)

        def send_hidden(k, inner):
            p = b * 8 + lax.rem(c + k, 8)
            piece = hid.at[:, pl.ds(pl.multiple_of(p * 16, 16), 16), :]

            @pl.when(p != c)
            def _():
                send(piece, hall.at[pl.ds(c * 2, 2)], fwd_s, fwd_r, {"config": p})

            @pl.when(p == c)
            def _():
                pltpu.make_async_copy(piece, hall.at[pl.ds(c * 2, 2)], fwd_r).start()

            return inner

        lax.fori_loop(0, 8, send_hidden, 0)
        return carry

    lax.fori_loop(0, 4, forward, 0)

    c32[...] = cot[...].astype(F32).reshape(1024, F)

    def cot_nodes(i, carry):
        rows = pl.ds(pl.multiple_of(i * 256, 256), 256)
        part = jnp.concatenate(
            [c32[pl.ds(i * 4 + k, 64, stride=16), :] for k in range(4)], axis=0
        ).astype(BF)
        cotn[rows, :] = part
        gmn[rows, :] = mm_nt(part, aw[3]).astype(BF)
        return carry

    lax.fori_loop(0, 4, cot_nodes, 0)

    hub_t[...] = hubw[...].astype(F32).T.astype(BF)
    for l in range(2):
        fa_t[0:F, l * 512 : (l + 1) * 512] = feat[l].astype(F32).T.astype(BF)
        fa_t[F : 2 * F, l * 512 : (l + 1) * 512] = agg[l].astype(F32).T.astype(BF)

    wait_bytes(hall, fwd_r)
    h32[...] = hall[...].astype(F32).reshape(1024, F)

    w_qkv = jnp.concatenate([aw[0], aw[1], aw[2]], axis=1)

    def head_of(shape, dim, width):
        return lax.broadcasted_iota(jnp.int32, shape, dim) // width

    head_mask = jnp.where(
        head_of((256, F), 0, 64) == head_of((256, F), 1, 32), 1.0, 0.0
    ).astype(BF)
    ones_mm = jnp.where(
        head_of((256, 256), 0, 64) == head_of((256, 256), 1, 64), 1.0, 0.0
    ).astype(BF)
    ones_dm = jnp.where(
        head_of((F, 256), 0, 32) == head_of((F, 256), 1, 64), 1.0, 0.0
    ).astype(BF)
    lane = lax.broadcasted_iota(jnp.int32, (64, F), 1)

    def own_head(full):
        return jnp.where(
            lane < 64,
            jnp.where(lane < 32, full[0:64], full[64:128]),
            jnp.where(lane < 96, full[128:192], full[192:256]),
        )

    root = 1.0 / math.sqrt(32.0)

    def attend(i, carry):
        rows = pl.ds(pl.multiple_of(i * 256, 256), 256)
        h_four = jnp.concatenate([h32[pl.ds(i * 4 + k, 64, stride=16), :] for k in range(4)], axis=0)
        h_b = h_four.astype(BF)
        hn[rows, :] = h_b
        qkv = mm(h_b, w_qkv).astype(BF)
        mixes, d_q, d_k, d_v = [], [], [], []
        for k in range(4):
            q = qkv[k * 64 : (k + 1) * 64, 0:F]
            key = qkv[k * 64 : (k + 1) * 64, F : 2 * F]
            val = qkv[k * 64 : (k + 1) * 64, 2 * F : 3 * F]
            gm = gmn[pl.ds(pl.multiple_of(i * 256 + k * 64, 64), 64), :]
            key_x = jnp.concatenate([key] * 4, axis=0) * head_mask
            val_x = jnp.concatenate([val] * 4, axis=0) * head_mask
            t = jnp.tanh(mm_nt(q, key_x) * (root / CAP))
            w = jnp.exp(CAP * t)
            den = mm(w.astype(BF), ones_mm)
            p_b = (w / den).astype(BF)
            mix = mm(p_b, val_x)
            dp = mm_nt(gm, val_x)
            delta = mm((gm.astype(F32) * mix).astype(BF), ones_dm)
            ds = (p_b.astype(F32) * (dp - delta) * ((1.0 - t * t) * root)).astype(BF)
            mixes.append(mix.astype(BF))
            d_q.append(mm(ds, key_x).astype(BF))
            d_k.append(own_head(mm_tn(ds, q)).astype(BF))
            d_v.append(own_head(mm_tn(p_b, gm)).astype(BF))
        mix_b = jnp.concatenate(mixes, axis=0)
        mixn[rows, :] = mix_b
        grads = jnp.concatenate(
            [jnp.concatenate(d_q, axis=0), jnp.concatenate(d_k, axis=0), jnp.concatenate(d_v, axis=0)],
            axis=1,
        )
        dqkv[rows, :] = grads
        out = h_four + mm(mix_b, aw[3])
        back = cotn[rows, :].astype(F32) + mm_nt(grads, w_qkv)
        for k in range(4):
            o32[pl.ds(i * 4 + k, 64, stride=16), :] = out[k * 64 : (k + 1) * 64]
            g32[pl.ds(i * 4 + k, 64, stride=16), :] = back[k * 64 : (k + 1) * 64]
        return carry

    lax.fori_loop(0, 4, attend, 0)
    gsend[...] = g32[...].reshape(64, 16, F).astype(BF)

    def send_back(k, carry):
        p = lax.rem(c + k, n_c)
        send(
            gsend.at[pl.ds(p * 2, 2)],
            gback.at[:, pl.ds(pl.multiple_of(c * 16, 16), 16), :],
            back_s, back_r, {"config": p},
        )
        return carry

    pltpu.make_async_copy(
        gsend.at[pl.ds(c * 2, 2)], gback.at[:, pl.ds(pl.multiple_of(c * 16, 16), 16), :], back_r
    ).start()
    lax.fori_loop(1, n_c, send_back, 0)

    lo_out[...] = o32[...].reshape(64, 16, F).astype(BF)
    part_qkv = mm_tn(hn[...], dqkv[...])
    part_o = mm_tn(mixn[...], cotn[...])
    for i in range(3):
        ars_src[i * 8 : (i + 1) * 8] = part_qkv[:, i * F : (i + 1) * F].reshape(8, 16, F).astype(BF)
    ars_src[24:32] = part_o.reshape(8, 16, F).astype(BF)

    def send_attn(k, carry):
        p = lax.rem(c + k, n_c)
        send(ars_src.at[p], ars_buf.at[c], ars_s, ars_r, {"config": p})
        return carry

    pltpu.make_async_copy(ars_src.at[c], ars_buf.at[c], ars_r).start()
    lax.fori_loop(1, n_c, send_attn, 0)

    wait_bytes(gback, back_r)

    def backward(b, carry):
        rows = pl.ds(pl.multiple_of(b * 128, 128), 128)
        for l in range(2):
            gp = (gback[l, rows, :].astype(F32) * dsil[l, rows, :]).astype(BF)
            gpre[pl.ds(pl.multiple_of(l * 512 + b * 128, 128), 128), :] = gp
            both = mm_nt(gp, w_sage)
            tot32[rows, l * F : (l + 1) * F] = both[:, :F]
            gacat[rows, l * F : (l + 1) * F] = both[:, F:].astype(BF)
        return carry

    lax.fori_loop(0, 4, backward, 0)

    srs_src[...] = mm(fa_t[...], gpre[...]).reshape(16, 16, F).astype(BF)

    def send_sage(k, carry):
        q = lax.rem(c // 2 + k, 16)
        p = q * 2

        @pl.when(p != c)
        def _():
            send(srs_src.at[q], srs_buf.at[c], srs_s, srs_r, {"config": p})

        @pl.when(p == c)
        def _():
            pltpu.make_async_copy(srs_src.at[q], srs_buf.at[c], srs_r).start()

        return carry

    lax.fori_loop(0, 16, send_sage, 0)

    hub_part = mm(hub_t[...], gacat[...])
    hg_src[...] = jnp.concatenate(
        [hub_part[:, :F].reshape(16, 8, F), hub_part[:, F:].reshape(16, 8, F)], axis=1
    ).astype(BF)

    def send_hub_grad(k, carry):
        s = lax.rem(g + k, n_g)
        send(hg_src.at[s], hg_buf.at[g], hg_s, hg_r, {"graph": s})
        return carry

    pltpu.make_async_copy(hg_src.at[g], hg_buf.at[g], hg_r).start()
    lax.fori_loop(1, n_g, send_hub_grad, 0)

    wait_bytes(ars_buf, ars_r)
    aag_src[...] = jnp.sum(ars_buf[...].astype(F32), axis=0).astype(BF)
    pltpu.make_async_copy(aag_src, aag_buf.at[c], aag_r).start()

    def send_attn_sum(k, carry):
        send(aag_src, aag_buf.at[c], aag_s, aag_r, {"config": lax.rem(c + k, n_c)})
        return carry

    lax.fori_loop(1, n_c, send_attn_sum, 0)

    @pl.when(lax.rem(c, 2) == 0)
    def _():
        wait_bytes(srs_buf, srs_r)
        sag_src[...] = jnp.sum(srs_buf[...].astype(F32), axis=0).astype(BF)
        pltpu.make_async_copy(sag_src, sag_buf.at[c // 2], sag_r).start()

        def send_sage_sum(k, carry):
            send(sag_src, sag_buf.at[c // 2], sag_s, sag_r, {"config": lax.rem(c + k, n_c)})
            return carry

        lax.fori_loop(1, n_c, send_sage_sum, 0)

    def back_rows(b, carry):
        rows = pl.ds(pl.multiple_of(b * 128, 128), 128)
        tot32[rows, :] = tot32[rows, :] + mm(adj_t[rows, :], gacat[...])
        return carry

    lax.fori_loop(0, 4, back_rows, 0)

    lane_id = lax.broadcasted_iota(jnp.int32, (512, F), 1)
    node_id = lax.broadcasted_iota(jnp.int32, (512, F), 0)
    want_t = jnp.full((512, F), -1, jnp.int32)
    for j in range(8):
        want_t = jnp.where((lane_id == j) | (lane_id == j + 8), ids[j] - base, want_t)
    onehot_t = jnp.where(node_id == want_t, 1.0, 0.0).astype(BF)

    wait_bytes(hg_buf, hg_r)
    hub_sum = jnp.sum(hg_buf[...].astype(F32), axis=0)
    hub_both = jnp.concatenate([hub_sum[0:8], hub_sum[8:16]], axis=1)
    high = hub_both.astype(BF).astype(F32)
    hub_mat = jnp.concatenate([high, hub_both - high, jnp.zeros((112, 256), F32)], axis=0).astype(BF)
    total = (tot32[...] + mm(onehot_t, hub_mat)).astype(BF)
    gf_out[0] = total[:, :F]
    gf_out[1] = total[:, F:]

    scale = 1.0 / math.sqrt(64 * 512)
    wait_bytes(aag_buf, aag_r)
    for i in range(4):
        gw_out[0, 2 + i] = aag_buf[i * 8 : (i + 1) * 8].astype(F32).reshape(F, F) * scale
    wait_bytes(sag_buf, sag_r)
    for i in range(2):
        gw_out[0, i] = sag_buf[i * 8 : (i + 1) * 8].astype(F32).reshape(F, F) * scale

    wait_bytes(hub_all.at[pl.ds(0, 15)], hub_s)
    wait_bytes(hall.at[pl.ds(0, 62)], fwd_s)
    wait_bytes(gsend.at[pl.ds(0, 62)], back_s)
    wait_bytes(ars_buf.at[pl.ds(0, 31)], ars_s)
    wait_bytes(hg_buf.at[pl.ds(0, 15)], hg_s)
    wait_bytes(aag_buf.at[pl.ds(0, 31)], aag_s)

    @pl.when(lax.rem(c, 2) == 0)
    def _():
        wait_bytes(srs_buf.at[pl.ds(0, 15)], srs_s)
        wait_bytes(aag_buf.at[pl.ds(0, 31)], sag_s)

    @pl.when(lax.rem(c, 2) == 1)
    def _():
        wait_bytes(srs_buf.at[pl.ds(0, 16)], srs_s)


def local(features, cotangent, sage_weight, attn_weight, tile_vals, tile_dst, tile_src, tile_count, hub_ids, hub_weight):
    vmem = pl.BlockSpec(memory_space=pltpu.VMEM)
    smem = pl.BlockSpec(memory_space=pltpu.SMEM)
    v = pltpu.VMEM
    return pl.pallas_call(
        kernel,
        out_shape=(
            jax.ShapeDtypeStruct((64, 16, F), BF),
            jax.ShapeDtypeStruct((2, 512, F), BF),
            jax.ShapeDtypeStruct((1, 6, F, F), F32),
        ),
        in_specs=[vmem] * 5 + [smem] * 4 + [vmem],
        out_specs=(vmem, vmem, vmem),
        scratch_shapes=[
            v((512, 512), BF),
            v((512, 512), BF),
            v((128, 512), BF),
            v((256, 1024), BF),
            v((512, 256), F32),
            v((2, 512, F), F32),
            v((2, 512, F), BF),
            v((2, 512, F), BF),
            v((64, 16, F), BF),
            v((1024, F), F32),
            v((1024, F), F32),
            v((1024, F), F32),
            v((1024, F), F32),
            v((1024, 384), BF),
            v((1024, F), BF),
            v((1024, F), BF),
            v((1024, F), BF),
            v((1024, F), BF),
            v((64, 16, F), BF),
            v((2, 512, F), BF),
            v((1024, F), BF),
            v((512, 256), BF),
            v((512, 256), F32),
            v((16, F), BF),
            v((16, 16, F), BF),
            v((16, 16, F), BF),
            v((16, 16, F), BF),
            v((32, 16, F), BF),
            v((32, 16, F), BF),
            v((16, F), BF),
            v((32, 16, F), BF),
            v((16, 16, F), BF),
            v((32, 16, F), BF),
            v((16, F), BF),
            v((16, 16, F), BF),
        ]
        + [pltpu.SemaphoreType.DMA] * 16,
        compiler_params=pltpu.CompilerParams(
            collective_id=0, has_side_effects=True, vmem_limit_bytes=40 * 2**20
        ),
    )(features, cotangent, sage_weight, attn_weight, tile_vals, tile_dst, tile_src, tile_count, hub_ids, hub_weight)


def solution(mesh):
    return jax.shard_map(
        local,
        mesh=mesh,
        in_specs=(
            P("config", "graph", None),
            P(None, ("graph", "config"), None),
            P(),
            P(),
            P("graph", None, None),
            P("graph"),
            P("graph"),
            P("graph"),
            P("graph"),
            P("graph", None),
        ),
        out_specs=(
            P(None, ("graph", "config"), None),
            P("config", "graph", None),
            P("graph", None, None, None),
        ),
        check_vma=False,
    )
```

```python
import functools
import math

import jax
import jax.numpy as jnp
from jax import lax
from jax.experimental import pallas as pl
from jax.experimental.pallas import tpu as pltpu
from jax.sharding import PartitionSpec as P

HEADS = 4
CAP = 20.0
F = 128
MESH = pl.DeviceIdType.MESH
BF = jnp.bfloat16
F32 = jnp.float32


def mm(a, b):
    return jnp.dot(a, b, preferred_element_type=F32)


def mm_nt(a, b):
    return lax.dot_general(a, b, (((1,), (1,)), ((), ())), preferred_element_type=F32)


def mm_tn(a, b):
    return lax.dot_general(a, b, (((0,), (0,)), ((), ())), preferred_element_type=F32)


def kernel(
    feat_h, cot_h, sw_h, aw_h, tiles_h, dst, src, cnt, ids, hubw_h,
    lo_h, gf_h, gw_h,
    feat, cot, sw, aw, tiles, hubw, lo_out, gf_out, gw_out,
    adj, adj_t, hub_t, fa_t, acc32, dsil, agg, hid, hall, h32, c32, g32, o32,
    dqkv, hn, mixn, cotn, gmn, gsend, gback, gpre, gacat, tot32,
    hubloc, hub_all, hg_src, hg_buf, ars_src, ars_buf, aag_src, aag_buf,
    srs_src, srs_buf, sag_src, sag_buf,
    fwd_s, fwd_r, back_s, back_r, hub_s, hub_r, hg_s, hg_r,
    ars_s, ars_r, aag_s, aag_r, srs_s, srs_r, sag_s, sag_r, in_sem, out_sem,
):
    g = lax.axis_index("graph")
    c = lax.axis_index("config")
    n_g = lax.axis_size("graph")
    n_c = lax.axis_size("config")
    loads = [
        pltpu.make_async_copy(a, b, in_sem.at[i])
        for i, (a, b) in enumerate(
            ((feat_h, feat), (tiles_h, tiles), (hubw_h, hubw), (sw_h, sw), (cot_h, cot), (aw_h, aw))
        )
    ]
    for load in loads:
        load.start()
    barrier = pltpu.get_barrier_semaphore()

    def hello_config(k, carry):
        pl.semaphore_signal(barrier, inc=1, device_id={"config": lax.rem(c + k, n_c)}, device_id_type=MESH)
        return carry

    def hello_graph(k, carry):
        pl.semaphore_signal(barrier, inc=1, device_id={"graph": lax.rem(g + k, n_g)}, device_id_type=MESH)
        return carry

    lax.fori_loop(1, n_g, hello_graph, 0)
    lax.fori_loop(1, n_c, hello_config, 0)

    def send(src_ref, dst_ref, send_sem, recv_sem, where):
        pltpu.make_async_remote_copy(
            src_ref=src_ref, dst_ref=dst_ref, send_sem=send_sem, recv_sem=recv_sem,
            device_id=where, device_id_type=MESH,
        ).start()

    def keep(src_ref, dst_ref, sem):
        pltpu.make_async_copy(src_ref, dst_ref, sem).start()

    def wait_bytes(ref, sem):
        pltpu.make_async_copy(ref, ref, sem).wait()

    base = g * 512
    row = lax.broadcasted_iota(jnp.int32, (16, 512), 0)
    col = lax.broadcasted_iota(jnp.int32, (16, 512), 1)
    want = jnp.full((16, 512), -1, jnp.int32)
    for j in range(8):
        want = jnp.where(row == j, ids[j] - base, want)
    onehot = jnp.where(col == want, 1.0, 0.0).astype(BF)
    loads[0].wait()
    x_cat = jnp.concatenate([feat[0], feat[1]], axis=1)
    rows_hub = mm(onehot, x_cat)
    hubloc[...] = jnp.concatenate([rows_hub[:8, :F], rows_hub[:8, F:]], axis=0).astype(BF)

    pl.semaphore_wait(barrier, n_g + n_c - 2)

    keep(hubloc, hub_all.at[g], hub_r)

    def send_hub(k, carry):
        send(hubloc, hub_all.at[g], hub_s, hub_r, {"graph": lax.rem(g + k, n_g)})
        return carry

    lax.fori_loop(1, n_g, send_hub, 0)

    for load in loads[1:]:
        load.wait()

    def build(b, carry):
        at = pl.multiple_of(b * 128, 128)
        for s in range(4):
            acc = jnp.zeros((128, 128), F32)
            for t in range(12):
                live = (dst[t] == b) & (src[t] == s) & (t < cnt[0])
                acc = acc + jnp.where(live, 1.0, 0.0) * tiles[t].astype(F32)
            adj[pl.ds(at, 128), s * 128 : (s + 1) * 128] = acc.astype(BF)
            adj_t[s * 128 : (s + 1) * 128, pl.ds(at, 128)] = acc.T.astype(BF)
        return carry

    lax.fori_loop(0, 4, build, 0)

    def first(b, carry):
        rows = pl.ds(pl.multiple_of(b * 128, 128), 128)
        acc32[rows, :] = mm(adj[rows, :], jnp.concatenate([feat[0], feat[1]], axis=1))
        return carry

    lax.fori_loop(0, 4, first, 0)

    wait_bytes(hub_all, hub_r)
    hubs = hub_all[...].astype(F32).reshape(16, 2, 8, F)
    hub_cat = jnp.concatenate(
        [hubs[:, 0].reshape(128, F).astype(BF), hubs[:, 1].reshape(128, F).astype(BF)], axis=1
    )
    w_sage = sw[...].reshape(2 * F, F)

    def forward(i, carry):
        b = lax.rem(c // 8 + i, 4)
        rows = pl.ds(pl.multiple_of(b * 128, 128), 128)
        acc = acc32[rows, :] + mm(hubw[rows, :], hub_cat)
        for l in range(2):
            a_l = acc[:, l * F : (l + 1) * F].astype(BF)
            agg[l, rows, :] = a_l
            pre = mm(jnp.concatenate([feat[l, rows, :], a_l], axis=1), w_sage)
            sig = 1.0 / (1.0 + jnp.exp(-pre))
            dsil[l, rows, :] = sig * (1.0 + pre * (1.0 - sig))
            hid[l, rows, :] = (pre * sig).astype(BF)

        def send_hidden(k, inner):
            p = b * 8 + lax.rem(c + k, 8)
            piece = hid.at[:, pl.ds(pl.multiple_of(p * 16, 16), 16), :]

            @pl.when(p != c)
            def _():
                send(piece, hall.at[pl.ds(c * 2, 2)], fwd_s, fwd_r, {"config": p})

            @pl.when(p == c)
            def _():
                keep(piece, hall.at[pl.ds(c * 2, 2)], fwd_r)

            return inner

        lax.fori_loop(0, 8, send_hidden, 0)
        return carry

    lax.fori_loop(0, 4, forward, 0)

    c32[...] = cot[...].astype(F32).reshape(1024, F)

    def cot_nodes(i, carry):
        rows = pl.ds(pl.multiple_of(i * 256, 256), 256)
        part = jnp.concatenate(
            [c32[pl.ds(i * 4 + k, 64, stride=16), :] for k in range(4)], axis=0
        ).astype(BF)
        cotn[rows, :] = part
        gmn[rows, :] = mm_nt(part, aw[3]).astype(BF)
        return carry

    lax.fori_loop(0, 4, cot_nodes, 0)

    hub_t[...] = hubw[...].astype(F32).T.astype(BF)
    for l in range(2):
        fa_t[0:F, l * 512 : (l + 1) * 512] = feat[l].astype(F32).T.astype(BF)
        fa_t[F : 2 * F, l * 512 : (l + 1) * 512] = agg[l].astype(F32).T.astype(BF)

    wait_bytes(hall, fwd_r)
    h32[...] = hall[...].astype(F32).reshape(1024, F)

    w_qkv = jnp.concatenate([aw[0], aw[1], aw[2]], axis=1)

    def head_of(shape, dim, width):
        return lax.broadcasted_iota(jnp.int32, shape, dim) // width

    head_mask = jnp.where(
        head_of((256, F), 0, 64) == head_of((256, F), 1, 32), 1.0, 0.0
    ).astype(BF)
    zeros = jnp.zeros((64, F), BF)
    lane = lax.broadcasted_iota(jnp.int32, (64, F), 1)

    def own_head(full):
        return jnp.where(
            lane < 64,
            jnp.where(lane < 32, full[0:64], full[64:128]),
            jnp.where(lane < 96, full[128:192], full[192:256]),
        )

    root = 1.0 / math.sqrt(32.0)

    def attend(i, carry):
        rows = pl.ds(pl.multiple_of(i * 256, 256), 256)
        h_four = jnp.concatenate([h32[pl.ds(i * 4 + k, 64, stride=16), :] for k in range(4)], axis=0)
        h_b = h_four.astype(BF)
        hn[rows, :] = h_b
        qkv = mm(h_b, w_qkv).astype(BF)
        four = range(4)
        q = [qkv[k * 64 : (k + 1) * 64, 0:F] for k in four]
        key_x = [jnp.concatenate([qkv[k * 64 : (k + 1) * 64, F : 2 * F]] * 4, axis=0) * head_mask for k in four]
        val_x = [
            jnp.concatenate(
                [jnp.concatenate([qkv[k * 64 : (k + 1) * 64, 2 * F : 3 * F]] * 4, axis=0) * head_mask, head_mask],
                axis=1,
            )
            for k in four
        ]
        t = [jnp.tanh(mm_nt(q[k], key_x[k]) * (root / CAP)) for k in four]
        w = [jnp.exp(CAP * t[k]).astype(BF) for k in four]
        both = [mm(w[k], val_x[k]) for k in four]
        inv = [1.0 / both[k][:, F:] for k in four]
        mix = [both[k][:, :F] * inv[k] for k in four]
        gm = [gmn[pl.ds(pl.multiple_of(i * 256 + k * 64, 64), 64), :].astype(F32) * inv[k] for k in four]
        gm_b = [gm[k].astype(BF) for k in four]
        less = [(-(gm_b[k].astype(F32) * mix[k])).astype(BF) for k in four]
        dp = [mm_nt(jnp.concatenate([gm_b[k], less[k]], axis=1), val_x[k]) for k in four]
        ds = [(w[k].astype(F32) * dp[k] * ((1.0 - t[k] * t[k]) * root)).astype(BF) for k in four]
        d_q = [mm(ds[k], key_x[k]).astype(BF) for k in four]
        right = [
            jnp.concatenate(
                [jnp.concatenate([q[k], zeros], axis=1), jnp.concatenate([zeros, gm_b[k]], axis=1)], axis=0
            )
            for k in four
        ]
        d_kv = [mm_tn(jnp.concatenate([ds[k], w[k]], axis=0), right[k]) for k in four]
        d_k = [own_head(d_kv[k][:, :F]).astype(BF) for k in four]
        d_v = [own_head(d_kv[k][:, F:]).astype(BF) for k in four]
        mixes = [mix[k].astype(BF) for k in four]
        mix_b = jnp.concatenate(mixes, axis=0)
        mixn[rows, :] = mix_b
        grads = jnp.concatenate(
            [jnp.concatenate(d_q, axis=0), jnp.concatenate(d_k, axis=0), jnp.concatenate(d_v, axis=0)],
            axis=1,
        )
        dqkv[rows, :] = grads
        out = h_four + mm(mix_b, aw[3])
        back = cotn[rows, :].astype(F32) + mm_nt(grads, w_qkv)
        for k in range(4):
            o32[pl.ds(i * 4 + k, 64, stride=16), :] = out[k * 64 : (k + 1) * 64]
            g32[pl.ds(i * 4 + k, 64, stride=16), :] = back[k * 64 : (k + 1) * 64]
        return carry

    lax.fori_loop(0, 4, attend, 0)
    gsend[...] = g32[...].reshape(64, 16, F).astype(BF)

    def send_back(k, carry):
        p = lax.rem(c + k, n_c)
        send(
            gsend.at[pl.ds(p * 2, 2)],
            gback.at[:, pl.ds(pl.multiple_of(c * 16, 16), 16), :],
            back_s, back_r, {"config": p},
        )
        return carry

    keep(gsend.at[pl.ds(c * 2, 2)], gback.at[:, pl.ds(pl.multiple_of(c * 16, 16), 16), :], back_r)
    lax.fori_loop(1, n_c, send_back, 0)

    lo_out[...] = o32[...].reshape(64, 16, F).astype(BF)
    store_lo = pltpu.make_async_copy(lo_out, lo_h, out_sem.at[0])
    store_lo.start()
    part_qkv = mm_tn(hn[...], dqkv[...])
    part_o = mm_tn(mixn[...], cotn[...])
    for i in range(3):
        ars_src[i * 8 : (i + 1) * 8] = part_qkv[:, i * F : (i + 1) * F].reshape(8, 16, F).astype(BF)
    ars_src[24:32] = part_o.reshape(8, 16, F).astype(BF)

    def send_attn(k, carry):
        p = lax.rem(c + k, n_c)
        send(ars_src.at[p], ars_buf.at[c], ars_s, ars_r, {"config": p})
        return carry

    keep(ars_src.at[c], ars_buf.at[c], ars_r)
    lax.fori_loop(1, n_c, send_attn, 0)

    wait_bytes(gback, back_r)

    def backward(b, carry):
        rows = pl.ds(pl.multiple_of(b * 128, 128), 128)
        for l in range(2):
            gp = (gback[l, rows, :].astype(F32) * dsil[l, rows, :]).astype(BF)
            gpre[pl.ds(pl.multiple_of(l * 512 + b * 128, 128), 128), :] = gp
            both = mm_nt(gp, w_sage)
            tot32[rows, l * F : (l + 1) * F] = both[:, :F]
            gacat[rows, l * F : (l + 1) * F] = both[:, F:].astype(BF)
        return carry

    lax.fori_loop(0, 4, backward, 0)

    srs_src[...] = mm(fa_t[...], gpre[...]).reshape(16, 16, F).astype(BF)

    def send_sage(k, carry):
        q = lax.rem(c // 2 + k, 16)
        p = q * 2

        @pl.when(p != c)
        def _():
            send(srs_src.at[q], srs_buf.at[c], srs_s, srs_r, {"config": p})

        @pl.when(p == c)
        def _():
            keep(srs_src.at[q], srs_buf.at[c], srs_r)

        return carry

    lax.fori_loop(0, 16, send_sage, 0)

    hub_part = mm(hub_t[...], gacat[...])
    hg_src[...] = jnp.concatenate(
        [hub_part[:, :F].reshape(16, 8, F), hub_part[:, F:].reshape(16, 8, F)], axis=1
    ).astype(BF)

    def send_hub_grad(k, carry):
        s = lax.rem(g + k, n_g)
        send(hg_src.at[s], hg_buf.at[g], hg_s, hg_r, {"graph": s})
        return carry

    keep(hg_src.at[g], hg_buf.at[g], hg_r)
    lax.fori_loop(1, n_g, send_hub_grad, 0)

    wait_bytes(ars_buf, ars_r)
    aag_src[...] = jnp.sum(ars_buf[...].astype(F32), axis=0).astype(BF)
    keep(aag_src, aag_buf.at[c], aag_r)

    def send_attn_sum(k, carry):
        send(aag_src, aag_buf.at[c], aag_s, aag_r, {"config": lax.rem(c + k, n_c)})
        return carry

    lax.fori_loop(1, n_c, send_attn_sum, 0)

    @pl.when(lax.rem(c, 2) == 0)
    def _():
        wait_bytes(srs_buf, srs_r)
        sag_src[...] = jnp.sum(srs_buf[...].astype(F32), axis=0).astype(BF)
        keep(sag_src, sag_buf.at[c // 2], sag_r)

        def send_sage_sum(k, carry):
            send(sag_src, sag_buf.at[c // 2], sag_s, sag_r, {"config": lax.rem(c + k, n_c)})
            return carry

        lax.fori_loop(1, n_c, send_sage_sum, 0)

    def back_rows(b, carry):
        rows = pl.ds(pl.multiple_of(b * 128, 128), 128)
        tot32[rows, :] = tot32[rows, :] + mm(adj_t[rows, :], gacat[...])
        return carry

    lax.fori_loop(0, 4, back_rows, 0)

    lane_id = lax.broadcasted_iota(jnp.int32, (512, F), 1)
    node_id = lax.broadcasted_iota(jnp.int32, (512, F), 0)
    want_t = jnp.full((512, F), -1, jnp.int32)
    for j in range(8):
        want_t = jnp.where((lane_id == j) | (lane_id == j + 8), ids[j] - base, want_t)
    onehot_t = jnp.where(node_id == want_t, 1.0, 0.0).astype(BF)

    wait_bytes(hg_buf, hg_r)
    hub_sum = jnp.sum(hg_buf[...].astype(F32), axis=0)
    hub_both = jnp.concatenate([hub_sum[0:8], hub_sum[8:16]], axis=1)
    high = hub_both.astype(BF).astype(F32)
    hub_mat = jnp.concatenate([high, hub_both - high, jnp.zeros((112, 256), F32)], axis=0).astype(BF)
    total = (tot32[...] + mm(onehot_t, hub_mat)).astype(BF)
    gf_out[0] = total[:, :F]
    gf_out[1] = total[:, F:]
    store_gf = pltpu.make_async_copy(gf_out, gf_h, out_sem.at[1])
    store_gf.start()

    scale = 1.0 / math.sqrt(64 * 512)
    wait_bytes(aag_buf, aag_r)
    for i in range(4):
        gw_out[0, 2 + i] = aag_buf[i * 8 : (i + 1) * 8].astype(F32).reshape(F, F) * scale
    wait_bytes(sag_buf, sag_r)
    for i in range(2):
        gw_out[0, i] = sag_buf[i * 8 : (i + 1) * 8].astype(F32).reshape(F, F) * scale

    store_gw = pltpu.make_async_copy(gw_out, gw_h, out_sem.at[2])
    store_gw.start()

    wait_bytes(hub_all.at[pl.ds(0, 15)], hub_s)
    wait_bytes(hall.at[pl.ds(0, 62)], fwd_s)
    wait_bytes(gsend.at[pl.ds(0, 62)], back_s)
    wait_bytes(ars_buf.at[pl.ds(0, 31)], ars_s)
    wait_bytes(hg_buf.at[pl.ds(0, 15)], hg_s)
    wait_bytes(aag_buf.at[pl.ds(0, 31)], aag_s)

    @pl.when(lax.rem(c, 2) == 0)
    def _():
        wait_bytes(srs_buf.at[pl.ds(0, 15)], srs_s)
        wait_bytes(aag_buf.at[pl.ds(0, 31)], sag_s)

    @pl.when(lax.rem(c, 2) == 1)
    def _():
        wait_bytes(srs_buf.at[pl.ds(0, 16)], srs_s)

    store_lo.wait()
    store_gf.wait()
    store_gw.wait()


def local(features, cotangent, sage_weight, attn_weight, tile_vals, tile_dst, tile_src, tile_count, hub_ids, hub_weight):
    smem = pl.BlockSpec(memory_space=pltpu.SMEM)
    hbm = pl.BlockSpec(memory_space=pltpu.HBM)
    v = pltpu.VMEM
    return pl.pallas_call(
        kernel,
        out_shape=(
            jax.ShapeDtypeStruct((64, 16, F), BF),
            jax.ShapeDtypeStruct((2, 512, F), BF),
            jax.ShapeDtypeStruct((1, 6, F, F), F32),
        ),
        in_specs=[hbm] * 5 + [smem] * 4 + [hbm],
        out_specs=(hbm, hbm, hbm),
        scratch_shapes=[
            v((2, 512, F), BF),
            v((64, 16, F), BF),
            v((2, F, F), BF),
            v((4, F, F), BF),
            v((12, F, F), BF),
            v((512, F), BF),
            v((64, 16, F), BF),
            v((2, 512, F), BF),
            v((1, 6, F, F), F32),
            v((512, 512), BF),
            v((512, 512), BF),
            v((128, 512), BF),
            v((256, 1024), BF),
            v((512, 256), F32),
            v((2, 512, F), F32),
            v((2, 512, F), BF),
            v((2, 512, F), BF),
            v((64, 16, F), BF),
            v((1024, F), F32),
            v((1024, F), F32),
            v((1024, F), F32),
            v((1024, F), F32),
            v((1024, 384), BF),
            v((1024, F), BF),
            v((1024, F), BF),
            v((1024, F), BF),
            v((1024, F), BF),
            v((64, 16, F), BF),
            v((2, 512, F), BF),
            v((1024, F), BF),
            v((512, 256), BF),
            v((512, 256), F32),
            v((16, F), BF),
            v((16, 16, F), BF),
            v((16, 16, F), BF),
            v((16, 16, F), BF),
            v((32, 16, F), BF),
            v((32, 16, F), BF),
            v((16, F), BF),
            v((32, 16, F), BF),
            v((16, 16, F), BF),
            v((32, 16, F), BF),
            v((16, F), BF),
            v((16, 16, F), BF),
        ]
        + [pltpu.SemaphoreType.DMA] * 16
        + [pltpu.SemaphoreType.DMA((6,)), pltpu.SemaphoreType.DMA((3,))],
        compiler_params=pltpu.CompilerParams(
            collective_id=0, has_side_effects=True, vmem_limit_bytes=60 * 2**20
        ),
    )(features, cotangent, sage_weight, attn_weight, tile_vals, tile_dst, tile_src, tile_count, hub_ids, hub_weight)


def solution(mesh):
    return jax.shard_map(
        local,
        mesh=mesh,
        in_specs=(
            P("config", "graph", None),
            P(None, ("graph", "config"), None),
            P(),
            P(),
            P("graph", None, None),
            P("graph"),
            P("graph"),
            P("graph"),
            P("graph"),
            P("graph", None),
        ),
        out_specs=(
            P(None, ("graph", "config"), None),
            P("config", "graph", None),
            P("graph", None, None, None),
        ),
        check_vma=False,
    )
```

```python
import functools
import math

import jax
import jax.numpy as jnp
from jax import lax
from jax.experimental import pallas as pl
from jax.experimental.pallas import tpu as pltpu
from jax.sharding import PartitionSpec as P

HEADS = 4
CAP = 20.0
F = 128
MESH = pl.DeviceIdType.MESH
BF = jnp.bfloat16
F32 = jnp.float32


def mm(a, b):
    return jnp.dot(a, b, preferred_element_type=F32)


def mm_nt(a, b):
    return lax.dot_general(a, b, (((1,), (1,)), ((), ())), preferred_element_type=F32)


def mm_tn(a, b):
    return lax.dot_general(a, b, (((0,), (0,)), ((), ())), preferred_element_type=F32)


def kernel(
    feat_h, cot_h, sw_h, aw_h, tiles_h, dst_h, src_h, cnt_h, ids_h, hubw_h,
    lo_h, gf_h, ga_h, gs_h,
    feat, cot, sw, aw, tiles, hubw, dst, src, cnt, ids, lo_out, gf_out,
    adj, adj_t, hub_t, fa_t, acc32, dsil, agg, hsend, hall, h32, c32, g32, o32,
    dqkv, hn, mixn, cotn, gmn, gsend, gback, gpre, gacat, tot32,
    hubloc, hub_all, hg_src, hg_buf, ars_src, ars_buf, aag_src, aag_buf,
    srs_src, srs_buf, sag_src, sag_buf,
    fwd_s, fwd_r, back_s, back_r, hub_s, hub_r, hg_s, hg_r,
    ars_s, ars_r, aag_s, aag_r, srs_s, srs_r, sag_s, sag_r, in_sem, out_sem,
):
    g = lax.axis_index("graph")
    c = lax.axis_index("config")
    n_g = lax.axis_size("graph")
    n_c = lax.axis_size("config")
    loads = [
        pltpu.make_async_copy(a, b, in_sem.at[i])
        for i, (a, b) in enumerate(
            (
                (feat_h, feat), (ids_h, ids), (tiles_h, tiles), (dst_h, dst), (src_h, src),
                (cnt_h, cnt), (hubw_h, hubw), (sw_h, sw), (cot_h, cot), (aw_h, aw),
            )
        )
    ]
    for load in loads:
        load.start()
    barrier = pltpu.get_barrier_semaphore()

    def hello_config(k, carry):
        pl.semaphore_signal(barrier, inc=1, device_id={"config": lax.rem(c + k, n_c)}, device_id_type=MESH)
        return carry

    def hello_graph(k, carry):
        pl.semaphore_signal(barrier, inc=1, device_id={"graph": lax.rem(g + k, n_g)}, device_id_type=MESH)
        return carry

    def over_config(one):
        lax.fori_loop(12, n_c, one, 0)
        lax.fori_loop(1, 12, one, 0)

    over_config(hello_config)
    lax.fori_loop(1, n_g, hello_graph, 0)

    def send(src_ref, dst_ref, send_sem, recv_sem, where):
        pltpu.make_async_remote_copy(
            src_ref=src_ref, dst_ref=dst_ref, send_sem=send_sem, recv_sem=recv_sem,
            device_id=where, device_id_type=MESH,
        ).start()

    def keep(src_ref, dst_ref, sem):
        pltpu.make_async_copy(src_ref, dst_ref, sem).start()

    def wait_bytes(ref, sem):
        pltpu.make_async_copy(ref, ref, sem).wait()

    loads[0].wait()
    loads[1].wait()
    base = g * 512
    row = lax.broadcasted_iota(jnp.int32, (16, 512), 0)
    col = lax.broadcasted_iota(jnp.int32, (16, 512), 1)
    want = jnp.full((16, 512), -1, jnp.int32)
    for j in range(8):
        want = jnp.where(row == j, ids[j] - base, want)
    onehot = jnp.where(col == want, 1.0, 0.0).astype(BF)
    x_cat = jnp.concatenate([feat[0], feat[1]], axis=1)
    rows_hub = mm(onehot, x_cat)
    hubloc[...] = jnp.concatenate([rows_hub[:8, :F], rows_hub[:8, F:]], axis=0).astype(BF)

    pl.semaphore_wait(barrier, n_g + n_c - 2)

    keep(hubloc, hub_all.at[g], hub_r)

    def send_hub(k, carry):
        send(hubloc, hub_all.at[g], hub_s, hub_r, {"graph": lax.rem(g + k, n_g)})
        return carry

    lax.fori_loop(1, n_g, send_hub, 0)

    for load in loads[2:]:
        load.wait()

    def halves(block):
        groups = block.shape[0] // 16
        split = block.reshape(groups, 2, 8, block.shape[1])
        return [split[:, h].reshape(groups * 8, block.shape[1]) for h in range(2)]

    def build(pair, carry):
        for s in range(4):
            found = []
            for b_in in range(2):
                b = pair * 2 + b_in
                acc = jnp.zeros((128, 128), F32)
                for t in range(12):
                    live = (dst[t] == b) & (src[t] == s) & (t < cnt[0])
                    acc = acc + jnp.where(live, 1.0, 0.0) * tiles[t].astype(F32)
                adj[pl.ds(pl.multiple_of(b * 128, 128), 128), s * 128 : (s + 1) * 128] = acc.astype(BF)
                found.append(acc)
            split = halves(jnp.concatenate(found, axis=0))
            for h in range(2):
                columns = pl.ds(pl.multiple_of(h * 256 + pair * 128, 128), 128)
                adj_t[s * 128 : (s + 1) * 128, columns] = split[h].T.astype(BF)
        return carry

    lax.fori_loop(0, 2, build, 0)

    def first(b, carry):
        rows = pl.ds(pl.multiple_of(b * 128, 128), 128)
        acc32[rows, :] = mm(adj[rows, :], jnp.concatenate([feat[0], feat[1]], axis=1))
        return carry

    lax.fori_loop(0, 4, first, 0)

    wait_bytes(hub_all, hub_r)
    hubs = hub_all[...].astype(F32).reshape(16, 2, 8, F)
    hub_cat = jnp.concatenate(
        [hubs[:, 0].reshape(128, F).astype(BF), hubs[:, 1].reshape(128, F).astype(BF)], axis=1
    )
    w_sage = sw[...].reshape(2 * F, F)

    def to_half(h):
        def one(k, carry):
            p = lax.rem(c + k, n_c)
            send(hsend.at[h, p], hall.at[h, c], fwd_s.at[h], fwd_r.at[h], {"config": p})
            return carry

        return one

    def forward(i, carry):
        b = lax.rem(c // 8 + 2 + i, 4)
        rows = pl.ds(pl.multiple_of(b * 128, 128), 128)
        acc = acc32[rows, :] + mm(hubw[rows, :], hub_cat)
        hidden, slope = [], []
        for l in range(2):
            a_l = acc[:, l * F : (l + 1) * F].astype(BF)
            agg[l, rows, :] = a_l
            pre = mm(jnp.concatenate([feat[l, rows, :], a_l], axis=1), w_sage)
            sig = 1.0 / (1.0 + jnp.exp(-pre))
            slope.append(halves(sig * (1.0 + pre * (1.0 - sig))))
            hidden.append(halves(pre * sig))
        for h in range(2):
            for l in range(2):
                dsil[pl.ds(pl.multiple_of((h * 2 + l) * 256 + b * 64, 64), 64), :] = slope[l][h]
            hsend[h, pl.ds(b * 8, 8)] = jnp.concatenate(
                [hidden[0][h].reshape(8, 8, F), hidden[1][h].reshape(8, 8, F)], axis=1
            ).astype(BF)

        def send_hidden(k, inner):
            p = b * 8 + lax.rem(c + k, 8)

            @pl.when(p != c)
            def _():
                send(hsend.at[0, p], hall.at[0, c], fwd_s.at[0], fwd_r.at[0], {"config": p})

            return inner

        lax.fori_loop(0, 8, send_hidden, 0)
        return carry

    lax.fori_loop(0, 4, forward, 0)
    over_config(to_half(1))
    for h in range(2):
        keep(hsend.at[h, c], hall.at[h, c], fwd_r.at[h])

    c32[...] = cot[...].astype(F32).reshape(1024, F)

    def cot_nodes(i, carry):
        rows = pl.ds(pl.multiple_of(i * 256, 256), 256)
        part = jnp.concatenate(
            [c32[pl.ds(i * 4 + k, 64, stride=16), :] for k in range(4)], axis=0
        ).astype(BF)
        cotn[rows, :] = part
        gmn[rows, :] = mm_nt(part, aw[3]).astype(BF)
        return carry

    lax.fori_loop(0, 4, cot_nodes, 0)

    split_hub = halves(hubw[...].astype(F32))
    for h in range(2):
        hub_t[:, h * 256 : (h + 1) * 256] = split_hub[h].T.astype(BF)
    for l in range(2):
        split_feat = halves(feat[l].astype(F32))
        split_agg = halves(agg[l].astype(F32))
        for h in range(2):
            columns = slice((h * 2 + l) * 256, (h * 2 + l + 1) * 256)
            fa_t[0:F, columns] = split_feat[h].T.astype(BF)
            fa_t[F : 2 * F, columns] = split_agg[h].T.astype(BF)

    w_qkv = jnp.concatenate([aw[0], aw[1], aw[2]], axis=1)

    def head_of(shape, dim, width):
        return lax.broadcasted_iota(jnp.int32, shape, dim) // width

    head_mask = jnp.where(
        head_of((256, F), 0, 64) == head_of((256, F), 1, 32), 1.0, 0.0
    ).astype(BF)
    zeros = jnp.zeros((64, F), BF)
    lane = lax.broadcasted_iota(jnp.int32, (64, F), 1)

    def own_head(full):
        return jnp.where(
            lane < 64,
            jnp.where(lane < 32, full[0:64], full[64:128]),
            jnp.where(lane < 96, full[128:192], full[192:256]),
        )

    root = 1.0 / math.sqrt(32.0)

    def attend(i, carry):
        rows = pl.ds(pl.multiple_of(i * 256, 256), 256)
        start = (i // 2) * 512 + lax.rem(i, 2) * 4
        h_four = jnp.concatenate([h32[pl.ds(start + k, 64, stride=8), :] for k in range(4)], axis=0)
        h_b = h_four.astype(BF)
        hn[rows, :] = h_b
        qkv = mm(h_b, w_qkv).astype(BF)
        four = range(4)
        q = [qkv[k * 64 : (k + 1) * 64, 0:F] for k in four]
        key_x = [jnp.concatenate([qkv[k * 64 : (k + 1) * 64, F : 2 * F]] * 4, axis=0) * head_mask for k in four]
        val_x = [
            jnp.concatenate(
                [jnp.concatenate([qkv[k * 64 : (k + 1) * 64, 2 * F : 3 * F]] * 4, axis=0) * head_mask, head_mask],
                axis=1,
            )
            for k in four
        ]
        t = [jnp.tanh(mm_nt(q[k], key_x[k]) * (root / CAP)) for k in four]
        w = [jnp.exp(CAP * t[k]).astype(BF) for k in four]
        both = [mm(w[k], val_x[k]) for k in four]
        inv = [1.0 / both[k][:, F:] for k in four]
        mix = [both[k][:, :F] * inv[k] for k in four]
        gm = [gmn[pl.ds(pl.multiple_of(i * 256 + k * 64, 64), 64), :].astype(F32) * inv[k] for k in four]
        gm_b = [gm[k].astype(BF) for k in four]
        less = [(-(gm_b[k].astype(F32) * mix[k])).astype(BF) for k in four]
        dp = [mm_nt(jnp.concatenate([gm_b[k], less[k]], axis=1), val_x[k]) for k in four]
        ds = [(w[k].astype(F32) * dp[k] * ((1.0 - t[k] * t[k]) * root)).astype(BF) for k in four]
        d_q = [mm(ds[k], key_x[k]).astype(BF) for k in four]
        right = [
            jnp.concatenate(
                [jnp.concatenate([q[k], zeros], axis=1), jnp.concatenate([zeros, gm_b[k]], axis=1)], axis=0
            )
            for k in four
        ]
        d_kv = [mm_tn(jnp.concatenate([ds[k], w[k]], axis=0), right[k]) for k in four]
        d_k = [own_head(d_kv[k][:, :F]).astype(BF) for k in four]
        d_v = [own_head(d_kv[k][:, F:]).astype(BF) for k in four]
        mixes = [mix[k].astype(BF) for k in four]
        mix_b = jnp.concatenate(mixes, axis=0)
        mixn[rows, :] = mix_b
        grads = jnp.concatenate(
            [jnp.concatenate(d_q, axis=0), jnp.concatenate(d_k, axis=0), jnp.concatenate(d_v, axis=0)],
            axis=1,
        )
        dqkv[rows, :] = grads
        out = h_four + mm(mix_b, aw[3])
        back = cotn[rows, :].astype(F32) + mm_nt(grads, w_qkv)
        for k in range(4):
            o32[pl.ds(i * 4 + k, 64, stride=16), :] = out[k * 64 : (k + 1) * 64]
            g32[pl.ds(start + k, 64, stride=8), :] = back[k * 64 : (k + 1) * 64]
        return carry

    def half_of_nodes(h, carry):
        rows = pl.ds(pl.multiple_of(h * 512, 512), 512)
        wait_bytes(hall.at[h], fwd_r.at[h])
        h32[rows, :] = hall[h].astype(F32).reshape(512, F)
        lax.fori_loop(h * 2, h * 2 + 2, attend, 0)
        gsend[h] = g32[rows, :].reshape(32, 16, F).astype(BF)

        def send_back(k, inner):
            p = lax.rem(c + k, n_c)
            send(gsend.at[h, p], gback.at[h, c], back_s.at[h], back_r.at[h], {"config": p})
            return inner

        over_config(send_back)
        keep(gsend.at[h, c], gback.at[h, c], back_r.at[h])
        return carry

    lax.fori_loop(0, 2, half_of_nodes, 0)

    lo_out[...] = o32[...].reshape(64, 16, F).astype(BF)
    store_lo = pltpu.make_async_copy(lo_out, lo_h, out_sem.at[0])
    store_lo.start()
    part_qkv = mm_tn(hn[...], dqkv[...])
    part_o = mm_tn(mixn[...], cotn[...])
    for i in range(3):
        ars_src[i * 8 : (i + 1) * 8] = part_qkv[:, i * F : (i + 1) * F].reshape(8, 16, F).astype(BF)
    ars_src[24:32] = part_o.reshape(8, 16, F).astype(BF)

    def send_attn(k, carry):
        p = lax.rem(c + k, n_c)
        send(ars_src.at[p], ars_buf.at[c], ars_s, ars_r, {"config": p})
        return carry

    keep(ars_src.at[c], ars_buf.at[c], ars_r)
    lax.fori_loop(1, n_c, send_attn, 0)

    def slopes(h):
        wait_bytes(gback.at[h], back_r.at[h])
        arrived = gback[h].astype(F32).reshape(32, 2, 8, F)
        parts = []
        for l in range(2):
            rows = slice((h * 2 + l) * 256, (h * 2 + l + 1) * 256)
            parts.append((arrived[:, l].reshape(256, F) * dsil[rows, :]).astype(BF))
            gpre[rows, :] = parts[l]
        return parts

    def through_weights(h, parts):
        for l in range(2):
            both = mm_nt(parts[l], w_sage)
            tot32[:, h, :, l * F : (l + 1) * F] = both[:, :F].reshape(32, 8, F)
            gacat[h * 256 : (h + 1) * 256, l * F : (l + 1) * F] = both[:, F:].astype(BF)

    parts = slopes(0)
    through_weights(0, parts)
    sage_first = mm(fa_t[:, 0:512], gpre[0:512, :])
    hub_first = mm(hub_t[:, 0:256], gacat[0:256, :])
    parts = slopes(1)
    srs_src[...] = (sage_first + mm(fa_t[:, 512:1024], gpre[512:1024, :])).reshape(16, 16, F).astype(BF)

    def send_sage(k, carry):
        q = lax.rem(c // 2 + k, 16)
        p = q * 2

        @pl.when(p != c)
        def _():
            send(srs_src.at[q], srs_buf.at[c], srs_s, srs_r, {"config": p})

        @pl.when(p == c)
        def _():
            keep(srs_src.at[q], srs_buf.at[c], srs_r)

        return carry

    lax.fori_loop(0, 16, send_sage, 0)

    through_weights(1, parts)
    hub_part = hub_first + mm(hub_t[:, 256:512], gacat[256:512, :])
    hg_src[...] = jnp.concatenate(
        [hub_part[:, :F].reshape(16, 8, F), hub_part[:, F:].reshape(16, 8, F)], axis=1
    ).astype(BF)

    def send_hub_grad(k, carry):
        s = lax.rem(g + k, n_g)
        send(hg_src.at[s], hg_buf.at[g], hg_s, hg_r, {"graph": s})
        return carry

    keep(hg_src.at[g], hg_buf.at[g], hg_r)
    lax.fori_loop(1, n_g, send_hub_grad, 0)

    wait_bytes(ars_buf, ars_r)
    aag_src[...] = jnp.sum(ars_buf[...].astype(F32), axis=0).astype(BF)
    keep(aag_src, aag_buf.at[c], aag_r)

    def send_attn_sum(k, carry):
        send(aag_src, aag_buf.at[c], aag_s, aag_r, {"config": lax.rem(c + k, n_c)})
        return carry

    lax.fori_loop(1, n_c, send_attn_sum, 0)

    @pl.when(lax.rem(c, 2) == 0)
    def _():
        wait_bytes(srs_buf, srs_r)
        sag_src[...] = jnp.sum(srs_buf[...].astype(F32), axis=0).astype(BF)
        keep(sag_src, sag_buf.at[c // 2], sag_r)

        def send_sage_sum(k, carry):
            send(sag_src, sag_buf.at[c // 2], sag_s, sag_r, {"config": lax.rem(c + k, n_c)})
            return carry

        lax.fori_loop(1, n_c, send_sage_sum, 0)

    def back_rows(b, carry):
        rows = pl.ds(pl.multiple_of(b * 128, 128), 128)
        nodes = pl.ds(b * 8, 8)
        tot32[nodes] = tot32[nodes] + mm(adj_t[rows, :], gacat[...]).reshape(8, 2, 8, 256)
        return carry

    lax.fori_loop(0, 4, back_rows, 0)

    lane_id = lax.broadcasted_iota(jnp.int32, (512, F), 1)
    node_id = lax.broadcasted_iota(jnp.int32, (512, F), 0)
    want_t = jnp.full((512, F), -1, jnp.int32)
    for j in range(8):
        want_t = jnp.where((lane_id == j) | (lane_id == j + 8), ids[j] - base, want_t)
    onehot_t = jnp.where(node_id == want_t, 1.0, 0.0).astype(BF)

    wait_bytes(hg_buf, hg_r)
    hub_sum = jnp.sum(hg_buf[...].astype(F32), axis=0)
    hub_both = jnp.concatenate([hub_sum[0:8], hub_sum[8:16]], axis=1)
    high = hub_both.astype(BF).astype(F32)
    hub_mat = jnp.concatenate([high, hub_both - high, jnp.zeros((112, 256), F32)], axis=0).astype(BF)
    total = (tot32[...].reshape(512, 256) + mm(onehot_t, hub_mat)).astype(BF)
    gf_out[0] = total[:, :F]
    gf_out[1] = total[:, F:]
    store_gf = pltpu.make_async_copy(gf_out, gf_h, out_sem.at[1])
    store_gf.start()

    wait_bytes(aag_buf, aag_r)
    store_ga = pltpu.make_async_copy(aag_buf, ga_h, out_sem.at[2])
    store_ga.start()
    wait_bytes(sag_buf, sag_r)
    store_gs = pltpu.make_async_copy(sag_buf, gs_h, out_sem.at[3])
    store_gs.start()

    wait_bytes(hub_all.at[pl.ds(0, 15)], hub_s)
    for h in range(2):
        wait_bytes(hall.at[h, pl.ds(0, 31)], fwd_s.at[h])
        wait_bytes(gback.at[h, pl.ds(0, 31)], back_s.at[h])
    wait_bytes(ars_buf.at[pl.ds(0, 31)], ars_s)
    wait_bytes(hg_buf.at[pl.ds(0, 15)], hg_s)
    wait_bytes(aag_buf.at[pl.ds(0, 31)], aag_s)

    @pl.when(lax.rem(c, 2) == 0)
    def _():
        wait_bytes(srs_buf.at[pl.ds(0, 15)], srs_s)
        wait_bytes(aag_buf.at[pl.ds(0, 31)], sag_s)

    @pl.when(lax.rem(c, 2) == 1)
    def _():
        wait_bytes(srs_buf.at[pl.ds(0, 16)], srs_s)

    store_lo.wait()
    store_gf.wait()
    store_ga.wait()
    store_gs.wait()


def finish(lo_h, gf_h, ga_h, gs_h, lo_out, gf_out, gw_out, lo, gf, ga, gs, gw, in_sem, out_sem):
    loads = [
        pltpu.make_async_copy(a, b, in_sem.at[i])
        for i, (a, b) in enumerate(((lo_h, lo), (gf_h, gf), (ga_h, ga), (gs_h, gs)))
    ]
    stores = [
        pltpu.make_async_copy(a, b, out_sem.at[i])
        for i, (a, b) in enumerate(((lo, lo_out), (gf, gf_out), (gw, gw_out)))
    ]
    for load in loads:
        load.start()
    scale = 1.0 / math.sqrt(64 * 512)
    loads[2].wait()
    for i in range(4):
        gw[0, 2 + i] = ga[i * 8 : (i + 1) * 8].astype(F32).reshape(F, F) * scale
    loads[3].wait()
    for i in range(2):
        gw[0, i] = gs[i * 8 : (i + 1) * 8].astype(F32).reshape(F, F) * scale
    stores[2].start()
    for i in range(2):
        loads[i].wait()
        stores[i].start()
    for store in stores:
        store.wait()


def local(features, cotangent, sage_weight, attn_weight, tile_vals, tile_dst, tile_src, tile_count, hub_ids, hub_weight):
    hbm = pl.BlockSpec(memory_space=pltpu.HBM)
    v = pltpu.VMEM
    made = pl.pallas_call(
        kernel,
        out_shape=(
            jax.ShapeDtypeStruct((64, 16, F), BF),
            jax.ShapeDtypeStruct((2, 512, F), BF),
            jax.ShapeDtypeStruct((32, 16, F), BF),
            jax.ShapeDtypeStruct((16, 16, F), BF),
        ),
        in_specs=[hbm] * 10,
        out_specs=(hbm,) * 4,
        scratch_shapes=[
            v((2, 512, F), BF),
            v((64, 16, F), BF),
            v((2, F, F), BF),
            v((4, F, F), BF),
            v((12, F, F), BF),
            v((512, F), BF),
            pltpu.SMEM((12,), jnp.int32),
            pltpu.SMEM((12,), jnp.int32),
            pltpu.SMEM((1,), jnp.int32),
            pltpu.SMEM((8,), jnp.int32),
            v((64, 16, F), BF),
            v((2, 512, F), BF),
            v((512, 512), BF),
            v((512, 512), BF),
            v((128, 512), BF),
            v((256, 1024), BF),
            v((512, 256), F32),
            v((1024, F), F32),
            v((2, 512, F), BF),
            v((2, 32, 16, F), BF),
            v((2, 32, 16, F), BF),
            v((1024, F), F32),
            v((1024, F), F32),
            v((1024, F), F32),
            v((1024, F), F32),
            v((1024, 384), BF),
            v((1024, F), BF),
            v((1024, F), BF),
            v((1024, F), BF),
            v((1024, F), BF),
            v((2, 32, 16, F), BF),
            v((2, 32, 16, F), BF),
            v((1024, F), BF),
            v((512, 256), BF),
            v((32, 2, 8, 256), F32),
            v((16, F), BF),
            v((16, 16, F), BF),
            v((16, 16, F), BF),
            v((16, 16, F), BF),
            v((32, 16, F), BF),
            v((32, 16, F), BF),
            v((16, F), BF),
            v((32, 16, F), BF),
            v((16, 16, F), BF),
            v((32, 16, F), BF),
            v((16, F), BF),
            v((16, 16, F), BF),
        ]
        + [pltpu.SemaphoreType.DMA((2,))] * 4
        + [pltpu.SemaphoreType.DMA] * 12
        + [pltpu.SemaphoreType.DMA((10,)), pltpu.SemaphoreType.DMA((4,))],
        compiler_params=pltpu.CompilerParams(
            collective_id=0, has_side_effects=True, vmem_limit_bytes=60 * 2**20
        ),
    )(features, cotangent, sage_weight, attn_weight, tile_vals, tile_dst, tile_src, tile_count, hub_ids, hub_weight)
    return pl.pallas_call(
        finish,
        out_shape=(
            jax.ShapeDtypeStruct((64, 16, F), BF),
            jax.ShapeDtypeStruct((2, 512, F), BF),
            jax.ShapeDtypeStruct((1, 6, F, F), F32),
        ),
        in_specs=[hbm] * 4,
        out_specs=(hbm,) * 3,
        scratch_shapes=[
            v((64, 16, F), BF),
            v((2, 512, F), BF),
            v((32, 16, F), BF),
            v((16, 16, F), BF),
            v((1, 6, F, F), F32),
            pltpu.SemaphoreType.DMA((4,)),
            pltpu.SemaphoreType.DMA((3,)),
        ],
        compiler_params=pltpu.CompilerParams(vmem_limit_bytes=60 * 2**20),
    )(*made)


def solution(mesh):
    return jax.shard_map(
        local,
        mesh=mesh,
        in_specs=(
            P("config", "graph", None),
            P(None, ("graph", "config"), None),
            P(),
            P(),
            P("graph", None, None),
            P("graph"),
            P("graph"),
            P("graph"),
            P("graph"),
            P("graph", None),
        ),
        out_specs=(
            P(None, ("graph", "config"), None),
            P("config", "graph", None),
            P("graph", None, None, None),
        ),
        check_vma=False,
    )
```

```python
import functools
import math

import jax
import jax.numpy as jnp
from jax import lax
from jax.experimental import pallas as pl
from jax.experimental.pallas import tpu as pltpu
from jax.sharding import PartitionSpec as P

HEADS = 4
CAP = 20.0
F = 128
MESH = pl.DeviceIdType.MESH
BF = jnp.bfloat16
F32 = jnp.float32


def mm(a, b):
    return jnp.dot(a, b, preferred_element_type=F32)


def mm_nt(a, b):
    return lax.dot_general(a, b, (((1,), (1,)), ((), ())), preferred_element_type=F32)


def mm_tn(a, b):
    return lax.dot_general(a, b, (((0,), (0,)), ((), ())), preferred_element_type=F32)


def kernel(
    feat_h, cot_h, sw_h, aw_h, tiles_h, dst_h, src_h, cnt_h, ids_h, hubw_h,
    lo_h, gf_h, ga_h, gs_h,
    feat, cot, sw, aw, tiles, hubw, dst, src, cnt, ids, lo_out, gf_out,
    adj, adj_t, hub_t, fa_t, acc32, dsil, agg, hsend, hall, h32, c32, g32, o32,
    dqkv, hn, mixn, cotn, gmn, gsend, gback, gpre, gacat, tot32,
    hubloc, hub_all, hg_src, hg_buf, ars_src, ars_buf, aag_src,
    srs_src, srs_buf, sag_src,
    fwd_s, fwd_r, back_s, back_r, hub_s, hub_r, hg_s, hg_r,
    ars_s, ars_r, aag_s, aag_r, srs_s, srs_r, sag_s, sag_r, in_sem, out_sem,
):
    g = lax.axis_index("graph")
    c = lax.axis_index("config")
    n_g = lax.axis_size("graph")
    n_c = lax.axis_size("config")
    barrier = pltpu.get_barrier_semaphore()

    def hello_config(k, carry):
        pl.semaphore_signal(barrier, inc=1, device_id={"config": lax.rem(c + k, n_c)}, device_id_type=MESH)
        return carry

    def hello_graph(k, carry):
        pl.semaphore_signal(barrier, inc=1, device_id={"graph": lax.rem(g + k, n_g)}, device_id_type=MESH)
        return carry

    def over_config(one):
        lax.fori_loop(12, n_c, one, 0)
        lax.fori_loop(1, 12, one, 0)

    over_config(hello_config)
    lax.fori_loop(1, n_g, hello_graph, 0)
    loads = [
        pltpu.make_async_copy(a, b, in_sem.at[i])
        for i, (a, b) in enumerate(
            (
                (feat_h, feat), (ids_h, ids), (tiles_h, tiles), (dst_h, dst), (src_h, src),
                (cnt_h, cnt), (hubw_h, hubw), (sw_h, sw), (cot_h, cot), (aw_h, aw),
            )
        )
    ]
    for load in loads:
        load.start()

    def send(src_ref, dst_ref, send_sem, recv_sem, where):
        pltpu.make_async_remote_copy(
            src_ref=src_ref, dst_ref=dst_ref, send_sem=send_sem, recv_sem=recv_sem,
            device_id=where, device_id_type=MESH,
        ).start()

    def keep(src_ref, dst_ref, sem):
        pltpu.make_async_copy(src_ref, dst_ref, sem).start()

    def wait_bytes(ref, sem):
        pltpu.make_async_copy(ref, ref, sem).wait()

    loads[0].wait()
    loads[1].wait()
    base = g * 512
    row = lax.broadcasted_iota(jnp.int32, (16, 512), 0)
    col = lax.broadcasted_iota(jnp.int32, (16, 512), 1)
    want = jnp.full((16, 512), -1, jnp.int32)
    for j in range(8):
        want = jnp.where(row == j, ids[j] - base, want)
    onehot = jnp.where(col == want, 1.0, 0.0).astype(BF)
    x_cat = jnp.concatenate([feat[0], feat[1]], axis=1)
    rows_hub = mm(onehot, x_cat)
    hubloc[...] = jnp.concatenate([rows_hub[:8, :F], rows_hub[:8, F:]], axis=0).astype(BF)

    pl.semaphore_wait(barrier, n_g + n_c - 2)

    keep(hubloc, hub_all.at[g], hub_r)

    def send_hub(k, carry):
        send(hubloc, hub_all.at[g], hub_s, hub_r, {"graph": lax.rem(g + k, n_g)})
        return carry

    lax.fori_loop(6, n_g, send_hub, 0)
    lax.fori_loop(1, 6, send_hub, 0)

    for load in loads[2:]:
        load.wait()

    def halves(block):
        groups = block.shape[0] // 16
        split = block.reshape(groups, 2, 8, block.shape[1])
        return [split[:, h].reshape(groups * 8, block.shape[1]) for h in range(2)]

    def build(pair, carry):
        for s in range(4):
            found = []
            for b_in in range(2):
                b = pair * 2 + b_in
                acc = jnp.zeros((128, 128), F32)
                for t in range(12):
                    live = (dst[t] == b) & (src[t] == s) & (t < cnt[0])
                    acc = acc + jnp.where(live, 1.0, 0.0) * tiles[t].astype(F32)
                adj[pl.ds(pl.multiple_of(b * 128, 128), 128), s * 128 : (s + 1) * 128] = acc.astype(BF)
                found.append(acc)
            split = halves(jnp.concatenate(found, axis=0))
            for h in range(2):
                columns = pl.ds(pl.multiple_of(h * 256 + pair * 128, 128), 128)
                adj_t[s * 128 : (s + 1) * 128, columns] = split[h].T.astype(BF)
        return carry

    lax.fori_loop(0, 2, build, 0)

    def first(b, carry):
        rows = pl.ds(pl.multiple_of(b * 128, 128), 128)
        acc32[rows, :] = mm(adj[rows, :], jnp.concatenate([feat[0], feat[1]], axis=1))
        return carry

    lax.fori_loop(0, 4, first, 0)

    wait_bytes(hub_all, hub_r)
    hubs = hub_all[...].astype(F32).reshape(16, 2, 8, F)
    hub_cat = jnp.concatenate(
        [hubs[:, 0].reshape(128, F).astype(BF), hubs[:, 1].reshape(128, F).astype(BF)], axis=1
    )
    w_sage = sw[...].reshape(2 * F, F)

    def to_half(h):
        def one(k, carry):
            p = lax.rem(c + k, n_c)
            send(hsend.at[h, p], hall.at[h, c], fwd_s.at[h], fwd_r.at[h], {"config": p})
            return carry

        return one

    def forward(i, carry):
        b = lax.rem(c // 8 + 2 + i, 4)
        rows = pl.ds(pl.multiple_of(b * 128, 128), 128)
        acc = acc32[rows, :] + mm(hubw[rows, :], hub_cat)
        hidden, slope = [], []
        for l in range(2):
            a_l = acc[:, l * F : (l + 1) * F].astype(BF)
            agg[l, rows, :] = a_l
            pre = mm(jnp.concatenate([feat[l, rows, :], a_l], axis=1), w_sage)
            sig = 1.0 / (1.0 + jnp.exp(-pre))
            slope.append(halves(sig * (1.0 + pre * (1.0 - sig))))
            hidden.append(halves(pre * sig))
        for h in range(2):
            for l in range(2):
                dsil[pl.ds(pl.multiple_of((h * 2 + l) * 256 + b * 64, 64), 64), :] = slope[l][h]
            hsend[h, pl.ds(b * 8, 8)] = jnp.concatenate(
                [hidden[0][h].reshape(8, 8, F), hidden[1][h].reshape(8, 8, F)], axis=1
            ).astype(BF)

        def send_hidden(k, inner):
            p = b * 8 + lax.rem(c + k, 8)

            @pl.when(p != c)
            def _():
                send(hsend.at[0, p], hall.at[0, c], fwd_s.at[0], fwd_r.at[0], {"config": p})

            return inner

        lax.fori_loop(0, 8, send_hidden, 0)
        return carry

    lax.fori_loop(0, 4, forward, 0)
    over_config(to_half(1))
    for h in range(2):
        keep(hsend.at[h, c], hall.at[h, c], fwd_r.at[h])

    c32[...] = cot[...].astype(F32).reshape(1024, F)

    def cot_nodes(i, carry):
        rows = pl.ds(pl.multiple_of(i * 256, 256), 256)
        part = jnp.concatenate(
            [c32[pl.ds(i * 4 + k, 64, stride=16), :] for k in range(4)], axis=0
        ).astype(BF)
        cotn[rows, :] = part
        gmn[rows, :] = mm_nt(part, aw[3]).astype(BF)
        return carry

    lax.fori_loop(0, 4, cot_nodes, 0)

    split_hub = halves(hubw[...].astype(F32))
    for h in range(2):
        hub_t[:, h * 256 : (h + 1) * 256] = split_hub[h].T.astype(BF)
    for l in range(2):
        split_feat = halves(feat[l].astype(F32))
        split_agg = halves(agg[l].astype(F32))
        for h in range(2):
            columns = slice((h * 2 + l) * 256, (h * 2 + l + 1) * 256)
            fa_t[0:F, columns] = split_feat[h].T.astype(BF)
            fa_t[F : 2 * F, columns] = split_agg[h].T.astype(BF)

    w_qkv = jnp.concatenate([aw[0], aw[1], aw[2]], axis=1)

    def head_of(shape, dim, width):
        return lax.broadcasted_iota(jnp.int32, shape, dim) // width

    head_mask = jnp.where(
        head_of((256, F), 0, 64) == head_of((256, F), 1, 32), 1.0, 0.0
    ).astype(BF)
    zeros = jnp.zeros((64, F), BF)
    lane = lax.broadcasted_iota(jnp.int32, (64, F), 1)

    def own_head(full):
        return jnp.where(
            lane < 64,
            jnp.where(lane < 32, full[0:64], full[64:128]),
            jnp.where(lane < 96, full[128:192], full[192:256]),
        )

    root = 1.0 / math.sqrt(32.0)

    def attend(i, carry):
        rows = pl.ds(pl.multiple_of(i * 256, 256), 256)
        start = (i // 2) * 512 + lax.rem(i, 2) * 4
        h_four = jnp.concatenate([h32[pl.ds(start + k, 64, stride=8), :] for k in range(4)], axis=0)
        h_b = h_four.astype(BF)
        hn[rows, :] = h_b
        qkv = mm(h_b, w_qkv).astype(BF)
        four = range(4)
        q = [qkv[k * 64 : (k + 1) * 64, 0:F] for k in four]
        key_x = [jnp.concatenate([qkv[k * 64 : (k + 1) * 64, F : 2 * F]] * 4, axis=0) * head_mask for k in four]
        val_x = [
            jnp.concatenate(
                [jnp.concatenate([qkv[k * 64 : (k + 1) * 64, 2 * F : 3 * F]] * 4, axis=0) * head_mask, head_mask],
                axis=1,
            )
            for k in four
        ]
        t = [jnp.tanh(mm_nt(q[k], key_x[k]) * (root / CAP)) for k in four]
        w = [jnp.exp(CAP * t[k]).astype(BF) for k in four]
        both = [mm(w[k], val_x[k]) for k in four]
        inv = [1.0 / both[k][:, F:] for k in four]
        mix = [both[k][:, :F] * inv[k] for k in four]
        gm = [gmn[pl.ds(pl.multiple_of(i * 256 + k * 64, 64), 64), :].astype(F32) * inv[k] for k in four]
        gm_b = [gm[k].astype(BF) for k in four]
        less = [(-(gm_b[k].astype(F32) * mix[k])).astype(BF) for k in four]
        dp = [mm_nt(jnp.concatenate([gm_b[k], less[k]], axis=1), val_x[k]) for k in four]
        ds = [(w[k].astype(F32) * dp[k] * ((1.0 - t[k] * t[k]) * root)).astype(BF) for k in four]
        d_q = [mm(ds[k], key_x[k]).astype(BF) for k in four]
        right = [
            jnp.concatenate(
                [jnp.concatenate([q[k], zeros], axis=1), jnp.concatenate([zeros, gm_b[k]], axis=1)], axis=0
            )
            for k in four
        ]
        d_kv = [mm_tn(jnp.concatenate([ds[k], w[k]], axis=0), right[k]) for k in four]
        d_k = [own_head(d_kv[k][:, :F]).astype(BF) for k in four]
        d_v = [own_head(d_kv[k][:, F:]).astype(BF) for k in four]
        mixes = [mix[k].astype(BF) for k in four]
        mix_b = jnp.concatenate(mixes, axis=0)
        mixn[rows, :] = mix_b
        grads = jnp.concatenate(
            [jnp.concatenate(d_q, axis=0), jnp.concatenate(d_k, axis=0), jnp.concatenate(d_v, axis=0)],
            axis=1,
        )
        dqkv[rows, :] = grads
        out = h_four + mm(mix_b, aw[3])
        back = cotn[rows, :].astype(F32) + mm_nt(grads, w_qkv)
        for k in range(4):
            o32[pl.ds(i * 4 + k, 64, stride=16), :] = out[k * 64 : (k + 1) * 64]
            g32[pl.ds(start + k, 64, stride=8), :] = back[k * 64 : (k + 1) * 64]
        return carry

    def half_of_nodes(h, carry):
        rows = pl.ds(pl.multiple_of(h * 512, 512), 512)
        wait_bytes(hall.at[h], fwd_r.at[h])
        h32[rows, :] = hall[h].astype(F32).reshape(512, F)
        lax.fori_loop(0, 2, lambda j, x: attend(h * 2 + j, x), 0, unroll=True)
        gsend[h] = g32[rows, :].reshape(32, 16, F).astype(BF)

        def send_back(k, inner):
            p = lax.rem(c + k, n_c)
            send(gsend.at[h, p], gback.at[h, c], back_s.at[h], back_r.at[h], {"config": p})
            return inner

        over_config(send_back)
        keep(gsend.at[h, c], gback.at[h, c], back_r.at[h])
        return carry

    lax.fori_loop(0, 2, half_of_nodes, 0)

    lo_out[...] = o32[...].reshape(64, 16, F).astype(BF)
    store_lo = pltpu.make_async_copy(lo_out, lo_h, out_sem.at[0])
    store_lo.start()
    part_qkv = mm_tn(hn[...], dqkv[...])
    part_o = mm_tn(mixn[...], cotn[...])
    for i in range(3):
        ars_src[i * 8 : (i + 1) * 8] = part_qkv[:, i * F : (i + 1) * F].reshape(8, 16, F).astype(BF)
    ars_src[24:32] = part_o.reshape(8, 16, F).astype(BF)

    def send_attn(k, carry):
        p = lax.rem(c + k, n_c)
        send(ars_src.at[p], ars_buf.at[c], ars_s, ars_r, {"config": p})
        return carry


    def slopes(h):
        wait_bytes(gback.at[h], back_r.at[h])
        arrived = gback[h].astype(F32).reshape(32, 2, 8, F)
        parts = []
        for l in range(2):
            rows = slice((h * 2 + l) * 256, (h * 2 + l + 1) * 256)
            parts.append((arrived[:, l].reshape(256, F) * dsil[rows, :]).astype(BF))
            gpre[rows, :] = parts[l]
        return parts

    def through_weights(h, parts):
        for l in range(2):
            both = mm_nt(parts[l], w_sage)
            tot32[:, h, :, l * F : (l + 1) * F] = both[:, :F].reshape(32, 8, F)
            gacat[h * 256 : (h + 1) * 256, l * F : (l + 1) * F] = both[:, F:].astype(BF)

    parts = slopes(0)
    through_weights(0, parts)
    sage_first = mm(fa_t[:, 0:512], gpre[0:512, :])
    hub_first = mm(hub_t[:, 0:256], gacat[0:256, :])
    keep(ars_src.at[c], ars_buf.at[c], ars_r)
    lax.fori_loop(1, n_c, send_attn, 0)
    parts = slopes(1)
    srs_src[...] = (sage_first + mm(fa_t[:, 512:1024], gpre[512:1024, :])).reshape(16, 16, F).astype(BF)

    def send_sage(k, carry):
        q = lax.rem(c // 2 + k, 16)
        p = q * 2 + lax.rem(q // 2, 2)

        @pl.when(p != c)
        def _():
            send(srs_src.at[q], srs_buf.at[c], srs_s, srs_r, {"config": p})

        @pl.when(p == c)
        def _():
            keep(srs_src.at[q], srs_buf.at[c], srs_r)

        return carry

    lax.fori_loop(0, 16, send_sage, 0)

    through_weights(1, parts)
    hub_part = hub_first + mm(hub_t[:, 256:512], gacat[256:512, :])
    hg_src[...] = jnp.concatenate(
        [hub_part[:, :F].reshape(16, 8, F), hub_part[:, F:].reshape(16, 8, F)], axis=1
    ).astype(BF)

    def send_hub_grad(k, carry):
        s = lax.rem(g + k, n_g)
        send(hg_src.at[s], hg_buf.at[g], hg_s, hg_r, {"graph": s})
        return carry

    keep(hg_src.at[g], hg_buf.at[g], hg_r)
    lax.fori_loop(1, n_g, send_hub_grad, 0)

    wait_bytes(ars_buf, ars_r)
    aag_src[...] = jnp.sum(ars_buf[...].astype(F32), axis=0).astype(BF)
    keep(aag_src, ga_h.at[c], aag_r)

    def send_attn_sum(k, carry):
        send(aag_src, ga_h.at[c], aag_s, aag_r, {"config": lax.rem(c + k, n_c)})
        return carry

    lax.fori_loop(1, n_c, send_attn_sum, 0)

    @pl.when(lax.rem(c, 2) == lax.rem(c // 4, 2))
    def _():
        wait_bytes(srs_buf, srs_r)
        sag_src[...] = jnp.sum(srs_buf[...].astype(F32), axis=0).astype(BF)
        keep(sag_src, gs_h.at[c // 2], sag_r)

        def send_sage_sum(k, carry):
            send(sag_src, gs_h.at[c // 2], sag_s, sag_r, {"config": lax.rem(c + k, n_c)})
            return carry

        lax.fori_loop(1, n_c, send_sage_sum, 0)

    def back_rows(b, carry):
        rows = pl.ds(pl.multiple_of(b * 128, 128), 128)
        nodes = pl.ds(b * 8, 8)
        tot32[nodes] = tot32[nodes] + mm(adj_t[rows, :], gacat[...]).reshape(8, 2, 8, 256)
        return carry

    lax.fori_loop(0, 4, back_rows, 0)

    lane_id = lax.broadcasted_iota(jnp.int32, (512, F), 1)
    node_id = lax.broadcasted_iota(jnp.int32, (512, F), 0)
    want_t = jnp.full((512, F), -1, jnp.int32)
    for j in range(8):
        want_t = jnp.where((lane_id == j) | (lane_id == j + 8), ids[j] - base, want_t)
    onehot_t = jnp.where(node_id == want_t, 1.0, 0.0).astype(BF)

    wait_bytes(hg_buf, hg_r)
    hub_sum = jnp.sum(hg_buf[...].astype(F32), axis=0)
    hub_both = jnp.concatenate([hub_sum[0:8], hub_sum[8:16]], axis=1)
    high = hub_both.astype(BF).astype(F32)
    hub_mat = jnp.concatenate([high, hub_both - high, jnp.zeros((112, 256), F32)], axis=0).astype(BF)
    total = (tot32[...].reshape(512, 256) + mm(onehot_t, hub_mat)).astype(BF)
    gf_out[0] = total[:, :F]
    gf_out[1] = total[:, F:]
    store_gf = pltpu.make_async_copy(gf_out, gf_h, out_sem.at[1])
    store_gf.start()

    wait_bytes(ga_h, aag_r)
    wait_bytes(gs_h, sag_r)

    wait_bytes(hub_all.at[pl.ds(0, 15)], hub_s)
    for h in range(2):
        wait_bytes(hall.at[h, pl.ds(0, 31)], fwd_s.at[h])
        wait_bytes(gback.at[h, pl.ds(0, 31)], back_s.at[h])
    wait_bytes(ars_buf.at[pl.ds(0, 31)], ars_s)
    wait_bytes(hg_buf.at[pl.ds(0, 15)], hg_s)
    wait_bytes(ars_buf.at[pl.ds(0, 31)], aag_s)

    @pl.when(lax.rem(c, 2) == lax.rem(c // 4, 2))
    def _():
        wait_bytes(srs_buf.at[pl.ds(0, 15)], srs_s)
        wait_bytes(ars_buf.at[pl.ds(0, 31)], sag_s)

    @pl.when(lax.rem(c, 2) != lax.rem(c // 4, 2))
    def _():
        wait_bytes(srs_buf.at[pl.ds(0, 16)], srs_s)

    store_lo.wait()
    store_gf.wait()


def finish(lo_h, gf_h, ga_h, gs_h, lo_out, gf_out, gw_out, lo, gf, ga, gs, gw, in_sem, out_sem):
    loads = [
        pltpu.make_async_copy(a, b, in_sem.at[i])
        for i, (a, b) in enumerate(((lo_h, lo), (gf_h, gf), (ga_h, ga), (gs_h, gs)))
    ]
    stores = [
        pltpu.make_async_copy(a, b, out_sem.at[i])
        for i, (a, b) in enumerate(((lo, lo_out), (gf, gf_out), (gw, gw_out)))
    ]
    for load in loads:
        load.start()
    scale = 1.0 / math.sqrt(64 * 512)
    loads[2].wait()
    for i in range(4):
        gw[0, 2 + i] = ga[i * 8 : (i + 1) * 8].astype(F32).reshape(F, F) * scale
    loads[3].wait()
    for i in range(2):
        gw[0, i] = gs[i * 8 : (i + 1) * 8].astype(F32).reshape(F, F) * scale
    stores[2].start()
    for i in range(2):
        loads[i].wait()
        stores[i].start()
    for store in stores:
        store.wait()


def local(features, cotangent, sage_weight, attn_weight, tile_vals, tile_dst, tile_src, tile_count, hub_ids, hub_weight):
    hbm = pl.BlockSpec(memory_space=pltpu.HBM)
    v = pltpu.VMEM
    made = pl.pallas_call(
        kernel,
        out_shape=(
            jax.ShapeDtypeStruct((64, 16, F), BF),
            jax.ShapeDtypeStruct((2, 512, F), BF),
            jax.ShapeDtypeStruct((32, 16, F), BF),
            jax.ShapeDtypeStruct((16, 16, F), BF),
        ),
        in_specs=[hbm] * 10,
        out_specs=(hbm,) * 4,
        scratch_shapes=[
            v((2, 512, F), BF),
            v((64, 16, F), BF),
            v((2, F, F), BF),
            v((4, F, F), BF),
            v((12, F, F), BF),
            v((512, F), BF),
            pltpu.SMEM((12,), jnp.int32),
            pltpu.SMEM((12,), jnp.int32),
            pltpu.SMEM((1,), jnp.int32),
            pltpu.SMEM((8,), jnp.int32),
            v((64, 16, F), BF),
            v((2, 512, F), BF),
            v((512, 512), BF),
            v((512, 512), BF),
            v((128, 512), BF),
            v((256, 1024), BF),
            v((512, 256), F32),
            v((1024, F), F32),
            v((2, 512, F), BF),
            v((2, 32, 16, F), BF),
            v((2, 32, 16, F), BF),
            v((1024, F), F32),
            v((1024, F), F32),
            v((1024, F), F32),
            v((1024, F), F32),
            v((1024, 384), BF),
            v((1024, F), BF),
            v((1024, F), BF),
            v((1024, F), BF),
            v((1024, F), BF),
            v((2, 32, 16, F), BF),
            v((2, 32, 16, F), BF),
            v((1024, F), BF),
            v((512, 256), BF),
            v((32, 2, 8, 256), F32),
            v((16, F), BF),
            v((16, 16, F), BF),
            v((16, 16, F), BF),
            v((16, 16, F), BF),
            v((32, 16, F), BF),
            v((32, 16, F), BF),
            v((16, F), BF),
            v((16, 16, F), BF),
            v((32, 16, F), BF),
            v((16, F), BF),
        ]
        + [pltpu.SemaphoreType.DMA((2,))] * 4
        + [pltpu.SemaphoreType.DMA] * 12
        + [pltpu.SemaphoreType.DMA((10,)), pltpu.SemaphoreType.DMA((2,))],
        compiler_params=pltpu.CompilerParams(
            collective_id=0, has_side_effects=True, vmem_limit_bytes=60 * 2**20
        ),
    )(features, cotangent, sage_weight, attn_weight, tile_vals, tile_dst, tile_src, tile_count, hub_ids, hub_weight)
    return pl.pallas_call(
        finish,
        out_shape=(
            jax.ShapeDtypeStruct((64, 16, F), BF),
            jax.ShapeDtypeStruct((2, 512, F), BF),
            jax.ShapeDtypeStruct((1, 6, F, F), F32),
        ),
        in_specs=[hbm] * 4,
        out_specs=(hbm,) * 3,
        scratch_shapes=[
            v((64, 16, F), BF),
            v((2, 512, F), BF),
            v((32, 16, F), BF),
            v((16, 16, F), BF),
            v((1, 6, F, F), F32),
            pltpu.SemaphoreType.DMA((4,)),
            pltpu.SemaphoreType.DMA((3,)),
        ],
        compiler_params=pltpu.CompilerParams(vmem_limit_bytes=60 * 2**20),
    )(*made)


def solution(mesh):
    return jax.shard_map(
        local,
        mesh=mesh,
        in_specs=(
            P("config", "graph", None),
            P(None, ("graph", "config"), None),
            P(),
            P(),
            P("graph", None, None),
            P("graph"),
            P("graph"),
            P("graph"),
            P("graph"),
            P("graph", None),
        ),
        out_specs=(
            P(None, ("graph", "config"), None),
            P("config", "graph", None),
            P("graph", None, None, None),
        ),
        check_vma=False,
    )
```

```python
import functools
import math

import jax
import jax.numpy as jnp
from jax import lax
from jax.experimental import pallas as pl
from jax.experimental.pallas import tpu as pltpu
from jax.sharding import PartitionSpec as P

HEADS = 4
CAP = 20.0
F = 128
MESH = pl.DeviceIdType.MESH
BF = jnp.bfloat16
F32 = jnp.float32


def mm(a, b):
    return jnp.dot(a, b, preferred_element_type=F32)


def mm_nt(a, b):
    return lax.dot_general(a, b, (((1,), (1,)), ((), ())), preferred_element_type=F32)


def mm_tn(a, b):
    return lax.dot_general(a, b, (((0,), (0,)), ((), ())), preferred_element_type=F32)


def kernel(
    feat_h, cot_h, sw_h, aw_h, tiles_h, dst_h, src_h, cnt_h, ids_h, hubw_h,
    lo_h, gf_h, ga_h, gs_h,
    feat, cot, sw, aw, tiles, hubw, dst, src, cnt, ids, lo_out, gf_out,
    adj, adj_t, hub_t, fa_t, acc32, dsil, agg, hsend, hall, h32, c32, g32, o32,
    dqkv, hn, mixn, cotn, gmn, gsend, gback, gpre, gacat, tot32,
    hubloc, hub_all, hg_src, hg_buf, ars_src, ars_buf, aag_src,
    srs_src, srs_buf, sag_src,
    fwd_s, fwd_r, back_s, back_r, hub_s, hub_r, hg_s, hg_r,
    ars_s, ars_r, aag_s, aag_r, srs_s, srs_r, sag_s, sag_r, in_sem, out_sem,
):
    g = lax.axis_index("graph")
    c = lax.axis_index("config")
    n_g = lax.axis_size("graph")
    n_c = lax.axis_size("config")
    barrier = pltpu.get_barrier_semaphore()

    def hello_config(k, carry):
        pl.semaphore_signal(barrier, inc=1, device_id={"config": lax.rem(c + k, n_c)}, device_id_type=MESH)
        return carry

    def hello_graph(k, carry):
        pl.semaphore_signal(barrier, inc=1, device_id={"graph": lax.rem(g + k, n_g)}, device_id_type=MESH)
        return carry

    def over_config(one):
        lax.fori_loop(12, n_c, one, 0)
        lax.fori_loop(1, 12, one, 0)

    over_config(hello_config)
    lax.fori_loop(1, n_g, hello_graph, 0)
    loads = [
        pltpu.make_async_copy(a, b, in_sem.at[i])
        for i, (a, b) in enumerate(
            (
                (feat_h, feat), (ids_h, ids), (tiles_h, tiles), (dst_h, dst), (src_h, src),
                (cnt_h, cnt), (hubw_h, hubw), (sw_h, sw), (cot_h, cot), (aw_h, aw),
            )
        )
    ]
    for load in loads:
        load.start()

    def send(src_ref, dst_ref, send_sem, recv_sem, where):
        pltpu.make_async_remote_copy(
            src_ref=src_ref, dst_ref=dst_ref, send_sem=send_sem, recv_sem=recv_sem,
            device_id=where, device_id_type=MESH,
        ).start()

    def keep(src_ref, dst_ref, sem):
        pltpu.make_async_copy(src_ref, dst_ref, sem).start()

    def wait_bytes(ref, sem):
        pltpu.make_async_copy(ref, ref, sem).wait()

    loads[0].wait()
    loads[1].wait()
    base = g * 512
    row = lax.broadcasted_iota(jnp.int32, (16, 512), 0)
    col = lax.broadcasted_iota(jnp.int32, (16, 512), 1)
    want = jnp.full((16, 512), -1, jnp.int32)
    for j in range(8):
        want = jnp.where(row == j, ids[j] - base, want)
    onehot = jnp.where(col == want, 1.0, 0.0).astype(BF)
    x_cat = jnp.concatenate([feat[0], feat[1]], axis=1)
    rows_hub = mm(onehot, x_cat)
    hubloc[...] = jnp.concatenate([rows_hub[:8, :F], rows_hub[:8, F:]], axis=0).astype(BF)

    pl.semaphore_wait(barrier, n_g + n_c - 2)

    keep(hubloc, hub_all.at[g], hub_r)

    def send_hub(k, carry):
        send(hubloc, hub_all.at[g], hub_s, hub_r, {"graph": lax.rem(g + k, n_g)})
        return carry

    lax.fori_loop(6, n_g, send_hub, 0)
    lax.fori_loop(1, 6, send_hub, 0)

    for load in loads[2:]:
        load.wait()

    def halves(block):
        groups = block.shape[0] // 16
        split = block.reshape(groups, 2, 8, block.shape[1])
        return [split[:, h].reshape(groups * 8, block.shape[1]) for h in range(2)]

    def build(pair, carry):
        for s in range(4):
            found = []
            for b_in in range(2):
                b = pair * 2 + b_in
                acc = jnp.zeros((128, 128), F32)
                for t in range(12):
                    live = (dst[t] == b) & (src[t] == s) & (t < cnt[0])
                    acc = acc + jnp.where(live, 1.0, 0.0) * tiles[t].astype(F32)
                adj[pl.ds(pl.multiple_of(b * 128, 128), 128), s * 128 : (s + 1) * 128] = acc.astype(BF)
                found.append(acc)
            split = halves(jnp.concatenate(found, axis=0))
            for h in range(2):
                columns = pl.ds(pl.multiple_of(h * 256 + pair * 128, 128), 128)
                adj_t[s * 128 : (s + 1) * 128, columns] = split[h].T.astype(BF)
        return carry

    lax.fori_loop(0, 2, build, 0)

    def first(b, carry):
        rows = pl.ds(pl.multiple_of(b * 128, 128), 128)
        acc32[rows, :] = mm(adj[rows, :], jnp.concatenate([feat[0], feat[1]], axis=1))
        return carry

    lax.fori_loop(0, 4, first, 0)

    wait_bytes(hub_all, hub_r)
    hubs = hub_all[...].astype(F32).reshape(16, 2, 8, F)
    hub_cat = jnp.concatenate(
        [hubs[:, 0].reshape(128, F).astype(BF), hubs[:, 1].reshape(128, F).astype(BF)], axis=1
    )
    w_sage = sw[...].reshape(2 * F, F)

    def to_half(h):
        def one(k, carry):
            p = lax.rem(c + k, n_c)
            send(hsend.at[h, p], hall.at[h, c], fwd_s.at[h], fwd_r.at[h], {"config": p})
            return carry

        return one

    def forward(i, carry):
        b = lax.rem(c // 8 + 2 + i, 4)
        rows = pl.ds(pl.multiple_of(b * 128, 128), 128)
        acc = acc32[rows, :] + mm(hubw[rows, :], hub_cat)
        hidden, slope = [], []
        for l in range(2):
            a_l = acc[:, l * F : (l + 1) * F].astype(BF)
            agg[l, rows, :] = a_l
            pre = mm(jnp.concatenate([feat[l, rows, :], a_l], axis=1), w_sage)
            sig = 0.5 + 0.5 * jnp.tanh(0.5 * pre)
            slope.append(halves(sig * (1.0 + pre * (1.0 - sig))))
            hidden.append(halves(pre * sig))
        for h in range(2):
            for l in range(2):
                dsil[pl.ds(pl.multiple_of((h * 2 + l) * 256 + b * 64, 64), 64), :] = slope[l][h]
            hsend[h, pl.ds(b * 8, 8)] = jnp.concatenate(
                [hidden[0][h].reshape(8, 8, F), hidden[1][h].reshape(8, 8, F)], axis=1
            ).astype(BF)

        def send_hidden(k, inner):
            p = b * 8 + lax.rem(c + k, 8)

            @pl.when(p != c)
            def _():
                send(hsend.at[0, p], hall.at[0, c], fwd_s.at[0], fwd_r.at[0], {"config": p})

            return inner

        lax.fori_loop(0, 8, send_hidden, 0)
        return carry

    lax.fori_loop(0, 4, forward, 0)
    over_config(to_half(1))
    for h in range(2):
        keep(hsend.at[h, c], hall.at[h, c], fwd_r.at[h])

    c32[...] = cot[...].astype(F32).reshape(1024, F)

    def cot_nodes(i, carry):
        rows = pl.ds(pl.multiple_of(i * 256, 256), 256)
        part = jnp.concatenate(
            [c32[pl.ds(i * 4 + k, 64, stride=16), :] for k in range(4)], axis=0
        ).astype(BF)
        cotn[rows, :] = part
        gmn[rows, :] = mm_nt(part, aw[3]).astype(BF)
        return carry

    lax.fori_loop(0, 4, cot_nodes, 0)

    split_hub = halves(hubw[...].astype(F32))
    for h in range(2):
        hub_t[:, h * 256 : (h + 1) * 256] = split_hub[h].T.astype(BF)
    for l in range(2):
        split_feat = halves(feat[l].astype(F32))
        split_agg = halves(agg[l].astype(F32))
        for h in range(2):
            columns = slice((h * 2 + l) * 256, (h * 2 + l + 1) * 256)
            fa_t[0:F, columns] = split_feat[h].T.astype(BF)
            fa_t[F : 2 * F, columns] = split_agg[h].T.astype(BF)

    w_qkv = jnp.concatenate([aw[0], aw[1], aw[2]], axis=1)

    def head_of(shape, dim, width):
        return lax.broadcasted_iota(jnp.int32, shape, dim) // width

    head_mask = jnp.where(
        head_of((256, F), 0, 64) == head_of((256, F), 1, 32), 1.0, 0.0
    ).astype(BF)
    zeros = jnp.zeros((64, F), BF)
    lane = lax.broadcasted_iota(jnp.int32, (64, F), 1)

    def own_head(full):
        return jnp.where(
            lane < 64,
            jnp.where(lane < 32, full[0:64], full[64:128]),
            jnp.where(lane < 96, full[128:192], full[192:256]),
        )

    root = 1.0 / math.sqrt(32.0)

    def attend(i, carry):
        rows = pl.ds(pl.multiple_of(i * 256, 256), 256)
        start = (i // 2) * 512 + lax.rem(i, 2) * 4
        h_four = jnp.concatenate([h32[pl.ds(start + k, 64, stride=8), :] for k in range(4)], axis=0)
        h_b = h_four.astype(BF)
        hn[rows, :] = h_b
        qkv = mm(h_b, w_qkv).astype(BF)
        four = range(4)
        q = [qkv[k * 64 : (k + 1) * 64, 0:F] for k in four]
        key_x = [jnp.concatenate([qkv[k * 64 : (k + 1) * 64, F : 2 * F]] * 4, axis=0) * head_mask for k in four]
        val_x = [
            jnp.concatenate(
                [jnp.concatenate([qkv[k * 64 : (k + 1) * 64, 2 * F : 3 * F]] * 4, axis=0) * head_mask, head_mask],
                axis=1,
            )
            for k in four
        ]
        t = [jnp.tanh(mm_nt(q[k], key_x[k]) * (root / CAP)) for k in four]
        w = [jnp.exp(CAP * t[k]).astype(BF) for k in four]
        both = [mm(w[k], val_x[k]) for k in four]
        inv = [1.0 / both[k][:, F:] for k in four]
        mix = [both[k][:, :F] * inv[k] for k in four]
        gm = [gmn[pl.ds(pl.multiple_of(i * 256 + k * 64, 64), 64), :].astype(F32) * inv[k] for k in four]
        gm_b = [gm[k].astype(BF) for k in four]
        less = jnp.concatenate([(gm_b[k].astype(F32) * mix[k]).astype(BF) for k in four], axis=0)
        less = mm_nt(less, head_mask)
        dp = [mm_nt(gm_b[k], val_x[k][:, :F]) - less[k * 64 : (k + 1) * 64] for k in four]
        ds = [(w[k].astype(F32) * dp[k] * ((1.0 - t[k] * t[k]) * root)).astype(BF) for k in four]
        d_q = [mm(ds[k], key_x[k]).astype(BF) for k in four]
        right = [
            jnp.concatenate(
                [jnp.concatenate([q[k], zeros], axis=1), jnp.concatenate([zeros, gm_b[k]], axis=1)], axis=0
            )
            for k in four
        ]
        d_kv = [mm_tn(jnp.concatenate([ds[k], w[k]], axis=0), right[k]) for k in four]
        d_k = [own_head(d_kv[k][:, :F]).astype(BF) for k in four]
        d_v = [own_head(d_kv[k][:, F:]).astype(BF) for k in four]
        mixes = [mix[k].astype(BF) for k in four]
        mix_b = jnp.concatenate(mixes, axis=0)
        mixn[rows, :] = mix_b
        grads = jnp.concatenate(
            [jnp.concatenate(d_q, axis=0), jnp.concatenate(d_k, axis=0), jnp.concatenate(d_v, axis=0)],
            axis=1,
        )
        dqkv[rows, :] = grads
        out = h_four + mm(mix_b, aw[3])
        back = cotn[rows, :].astype(F32) + mm_nt(grads, w_qkv)
        for k in range(4):
            o32[pl.ds(i * 4 + k, 64, stride=16), :] = out[k * 64 : (k + 1) * 64]
            g32[pl.ds(start + k, 64, stride=8), :] = back[k * 64 : (k + 1) * 64]
        return carry

    def half_of_nodes(h, carry):
        rows = pl.ds(pl.multiple_of(h * 512, 512), 512)
        wait_bytes(hall.at[h], fwd_r.at[h])
        h32[rows, :] = hall[h].astype(F32).reshape(512, F)
        lax.fori_loop(0, 2, lambda j, x: attend(h * 2 + j, x), 0, unroll=True)
        gsend[h] = g32[rows, :].reshape(32, 16, F).astype(BF)

        def send_back(k, inner):
            p = lax.rem(c + k, n_c)
            send(gsend.at[h, p], gback.at[h, c], back_s.at[h], back_r.at[h], {"config": p})
            return inner

        over_config(send_back)
        keep(gsend.at[h, c], gback.at[h, c], back_r.at[h])
        return carry

    lax.fori_loop(0, 2, half_of_nodes, 0)

    lo_out[...] = o32[...].reshape(64, 16, F).astype(BF)
    store_lo = pltpu.make_async_copy(lo_out, lo_h, out_sem.at[0])
    store_lo.start()
    part_qkv = mm_tn(hn[...], dqkv[...])
    part_o = mm_tn(mixn[...], cotn[...])
    for i in range(3):
        ars_src[i * 8 : (i + 1) * 8] = part_qkv[:, i * F : (i + 1) * F].reshape(8, 16, F).astype(BF)
    ars_src[24:32] = part_o.reshape(8, 16, F).astype(BF)

    def send_attn(k, carry):
        p = lax.rem(c + k, n_c)
        send(ars_src.at[p], ars_buf.at[c], ars_s, ars_r, {"config": p})
        return carry


    def slopes(h):
        wait_bytes(gback.at[h], back_r.at[h])
        arrived = gback[h].astype(F32).reshape(32, 2, 8, F)
        parts = []
        for l in range(2):
            rows = slice((h * 2 + l) * 256, (h * 2 + l + 1) * 256)
            parts.append((arrived[:, l].reshape(256, F) * dsil[rows, :]).astype(BF))
            gpre[rows, :] = parts[l]
        return parts

    def through_weights(h, parts):
        for l in range(2):
            both = mm_nt(parts[l], w_sage)
            tot32[:, h, :, l * F : (l + 1) * F] = both[:, :F].reshape(32, 8, F)
            gacat[h * 256 : (h + 1) * 256, l * F : (l + 1) * F] = both[:, F:].astype(BF)

    parts = slopes(0)
    through_weights(0, parts)
    sage_first = mm(fa_t[:, 0:512], gpre[0:512, :])
    hub_first = mm(hub_t[:, 0:256], gacat[0:256, :])
    keep(ars_src.at[c], ars_buf.at[c], ars_r)
    over_config(send_attn)
    parts = slopes(1)
    srs_src[...] = (sage_first + mm(fa_t[:, 512:1024], gpre[512:1024, :])).reshape(16, 16, F).astype(BF)

    def send_sage(k, carry):
        q = lax.rem(c // 2 + k, 16)
        p = q * 2 + lax.rem(q // 2, 2)

        @pl.when(p != c)
        def _():
            send(srs_src.at[q], srs_buf.at[c], srs_s, srs_r, {"config": p})

        @pl.when(p == c)
        def _():
            keep(srs_src.at[q], srs_buf.at[c], srs_r)

        return carry

    lax.fori_loop(6, 16, send_sage, 0)
    lax.fori_loop(0, 6, send_sage, 0)

    through_weights(1, parts)
    hub_part = hub_first + mm(hub_t[:, 256:512], gacat[256:512, :])
    hg_src[...] = jnp.concatenate(
        [hub_part[:, :F].reshape(16, 8, F), hub_part[:, F:].reshape(16, 8, F)], axis=1
    ).astype(BF)

    def send_hub_grad(k, carry):
        s = lax.rem(g + k, n_g)
        send(hg_src.at[s], hg_buf.at[g], hg_s, hg_r, {"graph": s})
        return carry

    keep(hg_src.at[g], hg_buf.at[g], hg_r)
    lax.fori_loop(6, n_g, send_hub_grad, 0)
    lax.fori_loop(1, 6, send_hub_grad, 0)

    wait_bytes(ars_buf, ars_r)
    aag_src[...] = jnp.sum(ars_buf[...].astype(F32), axis=0).astype(BF)
    keep(aag_src, ga_h.at[c], aag_r)

    def send_attn_sum(k, carry):
        send(aag_src, ga_h.at[c], aag_s, aag_r, {"config": lax.rem(c + k, n_c)})
        return carry

    over_config(send_attn_sum)

    @pl.when(lax.rem(c, 2) == lax.rem(c // 4, 2))
    def _():
        wait_bytes(srs_buf, srs_r)
        sag_src[...] = jnp.sum(srs_buf[...].astype(F32), axis=0).astype(BF)
        keep(sag_src, gs_h.at[c // 2], sag_r)

        def send_sage_sum(k, carry):
            send(sag_src, gs_h.at[c // 2], sag_s, sag_r, {"config": lax.rem(c + k, n_c)})
            return carry

        over_config(send_sage_sum)

    def back_rows(b, carry):
        rows = pl.ds(pl.multiple_of(b * 128, 128), 128)
        nodes = pl.ds(b * 8, 8)
        tot32[nodes] = tot32[nodes] + mm(adj_t[rows, :], gacat[...]).reshape(8, 2, 8, 256)
        return carry

    lax.fori_loop(0, 4, back_rows, 0)

    lane_id = lax.broadcasted_iota(jnp.int32, (512, F), 1)
    node_id = lax.broadcasted_iota(jnp.int32, (512, F), 0)
    want_t = jnp.full((512, F), -1, jnp.int32)
    for j in range(8):
        want_t = jnp.where((lane_id == j) | (lane_id == j + 8), ids[j] - base, want_t)
    onehot_t = jnp.where(node_id == want_t, 1.0, 0.0).astype(BF)

    wait_bytes(hg_buf, hg_r)
    hub_sum = jnp.sum(hg_buf[...].astype(F32), axis=0)
    hub_both = jnp.concatenate([hub_sum[0:8], hub_sum[8:16]], axis=1)
    high = hub_both.astype(BF).astype(F32)
    hub_mat = jnp.concatenate([high, hub_both - high, jnp.zeros((112, 256), F32)], axis=0).astype(BF)
    total = (tot32[...].reshape(512, 256) + mm(onehot_t, hub_mat)).astype(BF)
    gf_out[0] = total[:, :F]
    gf_out[1] = total[:, F:]
    store_gf = pltpu.make_async_copy(gf_out, gf_h, out_sem.at[1])
    store_gf.start()

    wait_bytes(ga_h, aag_r)
    wait_bytes(gs_h, sag_r)

    wait_bytes(hub_all.at[pl.ds(0, 15)], hub_s)
    for h in range(2):
        wait_bytes(hall.at[h, pl.ds(0, 31)], fwd_s.at[h])
        wait_bytes(gback.at[h, pl.ds(0, 31)], back_s.at[h])
    wait_bytes(ars_buf.at[pl.ds(0, 31)], ars_s)
    wait_bytes(hg_buf.at[pl.ds(0, 15)], hg_s)
    wait_bytes(ars_buf.at[pl.ds(0, 31)], aag_s)

    @pl.when(lax.rem(c, 2) == lax.rem(c // 4, 2))
    def _():
        wait_bytes(srs_buf.at[pl.ds(0, 15)], srs_s)
        wait_bytes(ars_buf.at[pl.ds(0, 31)], sag_s)

    @pl.when(lax.rem(c, 2) != lax.rem(c // 4, 2))
    def _():
        wait_bytes(srs_buf.at[pl.ds(0, 16)], srs_s)

    store_lo.wait()
    store_gf.wait()


def finish(lo_h, gf_h, ga_h, gs_h, lo_out, gf_out, gw_out, lo, gf, ga, gs, gw, in_sem, out_sem):
    loads = [pltpu.make_async_copy(ga_h, ga, in_sem.at[0]), pltpu.make_async_copy(gs_h, gs, in_sem.at[1])]
    stores = [pltpu.make_async_copy(gw.at[0, i], gw_out.at[0, i], out_sem.at[i]) for i in range(6)]
    for a_h, a, a_out, size in ((lo_h, lo, lo_out, 16), (gf_h, gf, gf_out, 1)):
        for i in range(a.shape[0] // size):
            part = pl.ds(i * size, size)
            loads.append(pltpu.make_async_copy(a_h.at[part], a.at[part], in_sem.at[len(loads)]))
            stores.append(pltpu.make_async_copy(a.at[part], a_out.at[part], out_sem.at[len(stores)]))
    for load in loads:
        load.start()
    scale = 1.0 / math.sqrt(64 * 512)
    loads[0].wait()
    for i in range(4):
        gw[0, 2 + i] = ga[i * 8 : (i + 1) * 8].astype(F32).reshape(F, F) * scale
        stores[2 + i].start()
    loads[1].wait()
    for i in range(2):
        gw[0, i] = gs[i * 8 : (i + 1) * 8].astype(F32).reshape(F, F) * scale
        stores[i].start()
    for load, store in zip(loads[2:], stores[6:]):
        load.wait()
        store.start()
    for store in stores:
        store.wait()


def local(features, cotangent, sage_weight, attn_weight, tile_vals, tile_dst, tile_src, tile_count, hub_ids, hub_weight):
    hbm = pl.BlockSpec(memory_space=pltpu.HBM)
    v = pltpu.VMEM
    made = pl.pallas_call(
        kernel,
        out_shape=(
            jax.ShapeDtypeStruct((64, 16, F), BF),
            jax.ShapeDtypeStruct((2, 512, F), BF),
            jax.ShapeDtypeStruct((32, 16, F), BF),
            jax.ShapeDtypeStruct((16, 16, F), BF),
        ),
        in_specs=[hbm] * 10,
        out_specs=(hbm,) * 4,
        scratch_shapes=[
            v((2, 512, F), BF),
            v((64, 16, F), BF),
            v((2, F, F), BF),
            v((4, F, F), BF),
            v((12, F, F), BF),
            v((512, F), BF),
            pltpu.SMEM((12,), jnp.int32),
            pltpu.SMEM((12,), jnp.int32),
            pltpu.SMEM((1,), jnp.int32),
            pltpu.SMEM((8,), jnp.int32),
            v((64, 16, F), BF),
            v((2, 512, F), BF),
            v((512, 512), BF),
            v((512, 512), BF),
            v((128, 512), BF),
            v((256, 1024), BF),
            v((512, 256), F32),
            v((1024, F), F32),
            v((2, 512, F), BF),
            v((2, 32, 16, F), BF),
            v((2, 32, 16, F), BF),
            v((1024, F), F32),
            v((1024, F), F32),
            v((1024, F), F32),
            v((1024, F), F32),
            v((1024, 384), BF),
            v((1024, F), BF),
            v((1024, F), BF),
            v((1024, F), BF),
            v((1024, F), BF),
            v((2, 32, 16, F), BF),
            v((2, 32, 16, F), BF),
            v((1024, F), BF),
            v((512, 256), BF),
            v((32, 2, 8, 256), F32),
            v((16, F), BF),
            v((16, 16, F), BF),
            v((16, 16, F), BF),
            v((16, 16, F), BF),
            v((32, 16, F), BF),
            v((32, 16, F), BF),
            v((16, F), BF),
            v((16, 16, F), BF),
            v((32, 16, F), BF),
            v((16, F), BF),
        ]
        + [pltpu.SemaphoreType.DMA((2,))] * 4
        + [pltpu.SemaphoreType.DMA] * 12
        + [pltpu.SemaphoreType.DMA((10,)), pltpu.SemaphoreType.DMA((2,))],
        compiler_params=pltpu.CompilerParams(
            collective_id=0, has_side_effects=True, vmem_limit_bytes=60 * 2**20
        ),
    )(features, cotangent, sage_weight, attn_weight, tile_vals, tile_dst, tile_src, tile_count, hub_ids, hub_weight)
    return pl.pallas_call(
        finish,
        out_shape=(
            jax.ShapeDtypeStruct((64, 16, F), BF),
            jax.ShapeDtypeStruct((2, 512, F), BF),
            jax.ShapeDtypeStruct((1, 6, F, F), F32),
        ),
        in_specs=[hbm] * 4,
        out_specs=(hbm,) * 3,
        scratch_shapes=[
            v((64, 16, F), BF),
            v((2, 512, F), BF),
            v((32, 16, F), BF),
            v((16, 16, F), BF),
            v((1, 6, F, F), F32),
            pltpu.SemaphoreType.DMA((8,)),
            pltpu.SemaphoreType.DMA((12,)),
        ],
        compiler_params=pltpu.CompilerParams(vmem_limit_bytes=60 * 2**20),
    )(*made)


def solution(mesh):
    return jax.shard_map(
        local,
        mesh=mesh,
        in_specs=(
            P("config", "graph", None),
            P(None, ("graph", "config"), None),
            P(),
            P(),
            P("graph", None, None),
            P("graph"),
            P("graph"),
            P("graph"),
            P("graph"),
            P("graph", None),
        ),
        out_specs=(
            P(None, ("graph", "config"), None),
            P("config", "graph", None),
            P("graph", None, None, None),
        ),
        check_vma=False,
    )
```

```python
import functools
import math

import jax
import jax.numpy as jnp
from jax import lax
from jax.experimental import pallas as pl
from jax.experimental.pallas import tpu as pltpu
from jax.sharding import PartitionSpec as P

HEADS = 4
CAP = 20.0
F = 128
MESH = pl.DeviceIdType.MESH
BF = jnp.bfloat16
F32 = jnp.float32


def mm(a, b):
    return jnp.dot(a, b, preferred_element_type=F32)


def mm_nt(a, b):
    return lax.dot_general(a, b, (((1,), (1,)), ((), ())), preferred_element_type=F32)


def mm_tn(a, b):
    return lax.dot_general(a, b, (((0,), (0,)), ((), ())), preferred_element_type=F32)


def kernel(
    feat_h, cot_h, sw_h, aw_h, tiles_h, dst_h, src_h, cnt_h, ids_h, hubw_h,
    lo_h, gf_h, ga_h, gs_h,
    feat, cot, sw, aw, tiles, hubw, dst, src, cnt, ids, lo_out, gf_out,
    adj, adj_t, hub_t, fa_t, acc32, dsil, agg, hsend, hall, h32, c32, g32, o32,
    dqkv, hn, mixn, cotn, gmn, gsend, gback, gpre, gacat, tot32,
    hubloc, hub_all, hg_src, hg_buf, ars_src, ars_buf, aag_src,
    srs_src, srs_buf, sag_src,
    fwd_s, fwd_r, back_s, back_r, hub_s, hub_r, hg_s, hg_r,
    ars_s, ars_r, aag_s, aag_r, srs_s, srs_r, sag_s, sag_r, in_sem, out_sem,
):
    g = lax.axis_index("graph")
    c = lax.axis_index("config")
    n_g = lax.axis_size("graph")
    n_c = lax.axis_size("config")
    barrier = pltpu.get_barrier_semaphore()

    def hello_config(k, carry):
        pl.semaphore_signal(barrier, inc=1, device_id={"config": lax.rem(c + k, n_c)}, device_id_type=MESH)
        return carry

    def hello_graph(k, carry):
        pl.semaphore_signal(barrier, inc=1, device_id={"graph": lax.rem(g + k, n_g)}, device_id_type=MESH)
        return carry

    def over_config(one):
        lax.fori_loop(12, n_c, one, 0)
        lax.fori_loop(1, 12, one, 0)

    over_config(hello_config)
    lax.fori_loop(1, n_g, hello_graph, 0)
    loads = [
        pltpu.make_async_copy(a, b, in_sem.at[i])
        for i, (a, b) in enumerate(
            (
                (feat_h, feat), (ids_h, ids), (tiles_h, tiles), (dst_h, dst), (src_h, src),
                (cnt_h, cnt), (hubw_h, hubw), (sw_h, sw), (cot_h, cot), (aw_h, aw),
            )
        )
    ]
    for load in loads:
        load.start()

    def send(src_ref, dst_ref, send_sem, recv_sem, where):
        pltpu.make_async_remote_copy(
            src_ref=src_ref, dst_ref=dst_ref, send_sem=send_sem, recv_sem=recv_sem,
            device_id=where, device_id_type=MESH,
        ).start()

    def keep(src_ref, dst_ref, sem):
        pltpu.make_async_copy(src_ref, dst_ref, sem).start()

    def wait_bytes(ref, sem):
        pltpu.make_async_copy(ref, ref, sem).wait()

    loads[0].wait()
    loads[1].wait()
    base = g * 512
    row = lax.broadcasted_iota(jnp.int32, (16, 512), 0)
    col = lax.broadcasted_iota(jnp.int32, (16, 512), 1)
    want = jnp.full((16, 512), -1, jnp.int32)
    for j in range(8):
        want = jnp.where(row == j, ids[j] - base, want)
    onehot = jnp.where(col == want, 1.0, 0.0).astype(BF)
    x_cat = jnp.concatenate([feat[0], feat[1]], axis=1)
    rows_hub = mm(onehot, x_cat)
    hubloc[...] = jnp.concatenate([rows_hub[:8, :F], rows_hub[:8, F:]], axis=0).astype(BF)

    pl.semaphore_wait(barrier, n_g + n_c - 2)

    keep(hubloc, hub_all.at[g], hub_r)

    def send_hub(k, carry):
        send(hubloc, hub_all.at[g], hub_s, hub_r, {"graph": lax.rem(g + k, n_g)})
        return carry

    lax.fori_loop(6, n_g, send_hub, 0)
    lax.fori_loop(1, 6, send_hub, 0)

    for load in loads[2:]:
        load.wait()

    def halves(block):
        groups = block.shape[0] // 16
        split = block.reshape(groups, 2, 8, block.shape[1])
        return [split[:, h].reshape(groups * 8, block.shape[1]) for h in range(2)]

    def build(pair, carry):
        for s in range(4):
            found = []
            for b_in in range(2):
                b = pair * 2 + b_in
                acc = jnp.zeros((128, 128), F32)
                for t in range(12):
                    live = (dst[t] == b) & (src[t] == s) & (t < cnt[0])
                    acc = acc + jnp.where(live, 1.0, 0.0) * tiles[t].astype(F32)
                adj[pl.ds(pl.multiple_of(b * 128, 128), 128), s * 128 : (s + 1) * 128] = acc.astype(BF)
                found.append(acc)
            split = halves(jnp.concatenate(found, axis=0))
            for h in range(2):
                columns = pl.ds(pl.multiple_of(h * 256 + pair * 128, 128), 128)
                adj_t[s * 128 : (s + 1) * 128, columns] = split[h].T.astype(BF)
        return carry

    lax.fori_loop(0, 2, build, 0)

    def first(b, carry):
        rows = pl.ds(pl.multiple_of(b * 128, 128), 128)
        acc32[rows, :] = mm(adj[rows, :], jnp.concatenate([feat[0], feat[1]], axis=1))
        return carry

    lax.fori_loop(0, 4, first, 0)

    wait_bytes(hub_all, hub_r)
    hubs = hub_all[...].astype(F32).reshape(16, 2, 8, F)
    hub_cat = jnp.concatenate(
        [hubs[:, 0].reshape(128, F).astype(BF), hubs[:, 1].reshape(128, F).astype(BF)], axis=1
    )
    w_sage = sw[...].reshape(2 * F, F)

    def to_half(h):
        def one(k, carry):
            p = lax.rem(c + k, n_c)
            send(hsend.at[h, p], hall.at[h, c], fwd_s.at[h], fwd_r.at[h], {"config": p})
            return carry

        return one

    def forward(i, carry):
        b = lax.rem(c // 8 + 2 + i, 4)
        rows = pl.ds(pl.multiple_of(b * 128, 128), 128)
        acc = acc32[rows, :] + mm(hubw[rows, :], hub_cat)
        hidden, slope = [], []
        for l in range(2):
            a_l = acc[:, l * F : (l + 1) * F].astype(BF)
            agg[l, rows, :] = a_l
            pre = mm(jnp.concatenate([feat[l, rows, :], a_l], axis=1), w_sage)
            sig = 0.5 + 0.5 * jnp.tanh(0.5 * pre)
            slope.append(halves(sig * (1.0 + pre * (1.0 - sig))))
            hidden.append(halves(pre * sig))
        for h in range(2):
            for l in range(2):
                dsil[pl.ds(pl.multiple_of((h * 2 + l) * 256 + b * 64, 64), 64), :] = slope[l][h]
            hsend[h, pl.ds(b * 8, 8)] = jnp.concatenate(
                [hidden[0][h].reshape(8, 8, F), hidden[1][h].reshape(8, 8, F)], axis=1
            ).astype(BF)

        def send_hidden(k, inner):
            p = b * 8 + lax.rem(c + k, 8)

            @pl.when(p != c)
            def _():
                send(hsend.at[0, p], hall.at[0, c], fwd_s.at[0], fwd_r.at[0], {"config": p})

            return inner

        lax.fori_loop(0, 8, send_hidden, 0)
        return carry

    lax.fori_loop(0, 4, forward, 0)
    over_config(to_half(1))
    for h in range(2):
        keep(hsend.at[h, c], hall.at[h, c], fwd_r.at[h])

    c32[...] = cot[...].astype(F32).reshape(1024, F)

    def cot_nodes(i, carry):
        rows = pl.ds(pl.multiple_of(i * 256, 256), 256)
        part = jnp.concatenate(
            [c32[pl.ds(i * 4 + k, 64, stride=16), :] for k in range(4)], axis=0
        ).astype(BF)
        cotn[rows, :] = part
        gmn[rows, :] = mm_nt(part, aw[3]).astype(BF)
        return carry

    lax.fori_loop(0, 4, cot_nodes, 0)

    split_hub = halves(hubw[...].astype(F32))
    for h in range(2):
        hub_t[:, h * 256 : (h + 1) * 256] = split_hub[h].T.astype(BF)
    for l in range(2):
        split_feat = halves(feat[l].astype(F32))
        split_agg = halves(agg[l].astype(F32))
        for h in range(2):
            columns = slice((h * 2 + l) * 256, (h * 2 + l + 1) * 256)
            fa_t[0:F, columns] = split_feat[h].T.astype(BF)
            fa_t[F : 2 * F, columns] = split_agg[h].T.astype(BF)

    w_qkv = jnp.concatenate([aw[0], aw[1], aw[2]], axis=1)

    def head_of(shape, dim, width):
        return lax.broadcasted_iota(jnp.int32, shape, dim) // width

    head_mask = jnp.where(
        head_of((256, F), 0, 64) == head_of((256, F), 1, 32), 1.0, 0.0
    ).astype(BF)
    zeros = jnp.zeros((64, F), BF)
    lane = lax.broadcasted_iota(jnp.int32, (64, F), 1)

    def own_head(full):
        return jnp.where(
            lane < 64,
            jnp.where(lane < 32, full[0:64], full[64:128]),
            jnp.where(lane < 96, full[128:192], full[192:256]),
        )

    root = 1.0 / math.sqrt(32.0)

    def attend(i, carry):
        rows = pl.ds(pl.multiple_of(i * 256, 256), 256)
        start = (i // 2) * 512 + lax.rem(i, 2) * 4
        h_b = jnp.concatenate([h32[pl.ds(start + k, 64, stride=8), :] for k in range(4)], axis=0).astype(BF)
        hn[rows, :] = h_b
        qkv = mm(h_b, w_qkv).astype(BF)
        four = range(4)
        q = [qkv[k * 64 : (k + 1) * 64, 0:F] for k in four]
        key_x = [jnp.concatenate([qkv[k * 64 : (k + 1) * 64, F : 2 * F]] * 4, axis=0) * head_mask for k in four]
        val_x = [
            jnp.concatenate(
                [jnp.concatenate([qkv[k * 64 : (k + 1) * 64, 2 * F : 3 * F]] * 4, axis=0) * head_mask, head_mask],
                axis=1,
            )
            for k in four
        ]
        t = [jnp.tanh(mm_nt(q[k], key_x[k]) * (root / CAP)) for k in four]
        w = [jnp.exp(CAP * t[k]).astype(BF) for k in four]
        both = [mm(w[k], val_x[k]) for k in four]
        inv = [1.0 / both[k][:, F:] for k in four]
        mix = [both[k][:, :F] * inv[k] for k in four]
        gm = [gmn[pl.ds(pl.multiple_of(i * 256 + k * 64, 64), 64), :].astype(F32) * inv[k] for k in four]
        gm_b = [gm[k].astype(BF) for k in four]
        less = jnp.concatenate([(gm_b[k].astype(F32) * mix[k]).astype(BF) for k in four], axis=0)
        less = mm_nt(less, head_mask)
        dp = [mm_nt(gm_b[k], val_x[k][:, :F]) - less[k * 64 : (k + 1) * 64] for k in four]
        ds = [(w[k].astype(F32) * dp[k] * ((1.0 - t[k] * t[k]) * root)).astype(BF) for k in four]
        d_q = [mm(ds[k], key_x[k]).astype(BF) for k in four]
        right = [
            jnp.concatenate(
                [jnp.concatenate([q[k], zeros], axis=1), jnp.concatenate([zeros, gm_b[k]], axis=1)], axis=0
            )
            for k in four
        ]
        d_kv = [mm_tn(jnp.concatenate([ds[k], w[k]], axis=0), right[k]) for k in four]
        d_k = [own_head(d_kv[k][:, :F]).astype(BF) for k in four]
        d_v = [own_head(d_kv[k][:, F:]).astype(BF) for k in four]
        mixes = [mix[k].astype(BF) for k in four]
        mix_b = jnp.concatenate(mixes, axis=0)
        mixn[rows, :] = mix_b
        grads = jnp.concatenate(
            [jnp.concatenate(d_q, axis=0), jnp.concatenate(d_k, axis=0), jnp.concatenate(d_v, axis=0)],
            axis=1,
        )
        dqkv[rows, :] = grads
        back = cotn[rows, :].astype(F32) + mm_nt(grads, w_qkv)
        for k in range(4):
            g32[pl.ds(start + k, 64, stride=8), :] = back[k * 64 : (k + 1) * 64]
        return carry

    def half_of_nodes(h, carry):
        rows = pl.ds(pl.multiple_of(h * 512, 512), 512)
        wait_bytes(hall.at[h], fwd_r.at[h])
        h32[rows, :] = hall[h].astype(F32).reshape(512, F)
        lax.fori_loop(0, 2, lambda j, x: attend(h * 2 + j, x), 0, unroll=True)
        gsend[h] = g32[rows, :].reshape(32, 16, F).astype(BF)

        def send_back(k, inner):
            p = lax.rem(c + k, n_c)
            send(gsend.at[h, p], gback.at[h, c], back_s.at[h], back_r.at[h], {"config": p})
            return inner

        over_config(send_back)
        keep(gsend.at[h, c], gback.at[h, c], back_r.at[h])
        return carry

    lax.fori_loop(0, 2, half_of_nodes, 0)

    def outputs(i, carry):
        rows = pl.ds(pl.multiple_of(i * 256, 256), 256)
        out = hn[rows, :].astype(F32) + mm(mixn[rows, :], aw[3])
        for k in range(4):
            o32[pl.ds(i * 4 + k, 64, stride=16), :] = out[k * 64 : (k + 1) * 64]
        return carry

    lax.fori_loop(0, 4, outputs, 0)
    lo_out[...] = o32[...].reshape(64, 16, F).astype(BF)
    store_lo = pltpu.make_async_copy(lo_out, lo_h, out_sem.at[0])
    store_lo.start()
    part_qkv = mm_tn(hn[...], dqkv[...])
    part_o = mm_tn(mixn[...], cotn[...])
    for i in range(3):
        ars_src[i * 8 : (i + 1) * 8] = part_qkv[:, i * F : (i + 1) * F].reshape(8, 16, F).astype(BF)
    ars_src[24:32] = part_o.reshape(8, 16, F).astype(BF)

    def send_attn(k, carry):
        p = lax.rem(c + k, n_c)
        send(ars_src.at[p], ars_buf.at[c], ars_s, ars_r, {"config": p})
        return carry


    def slopes(h):
        wait_bytes(gback.at[h], back_r.at[h])
        arrived = gback[h].astype(F32).reshape(32, 2, 8, F)
        parts = []
        for l in range(2):
            rows = slice((h * 2 + l) * 256, (h * 2 + l + 1) * 256)
            parts.append((arrived[:, l].reshape(256, F) * dsil[rows, :]).astype(BF))
            gpre[rows, :] = parts[l]
        return parts

    def through_weights(h, parts):
        for l in range(2):
            both = mm_nt(parts[l], w_sage)
            tot32[:, h, :, l * F : (l + 1) * F] = both[:, :F].reshape(32, 8, F)
            gacat[h * 256 : (h + 1) * 256, l * F : (l + 1) * F] = both[:, F:].astype(BF)

    parts = slopes(0)
    through_weights(0, parts)
    sage_first = mm(fa_t[:, 0:512], gpre[0:512, :])
    hub_first = mm(hub_t[:, 0:256], gacat[0:256, :])
    keep(ars_src.at[c], ars_buf.at[c], ars_r)
    over_config(send_attn)
    parts = slopes(1)
    srs_src[...] = (sage_first + mm(fa_t[:, 512:1024], gpre[512:1024, :])).reshape(16, 16, F).astype(BF)

    def send_sage(k, carry):
        q = lax.rem(c // 2 + k, 16)
        p = q * 2 + lax.rem(q // 2, 2)

        @pl.when(p != c)
        def _():
            send(srs_src.at[q], srs_buf.at[c], srs_s, srs_r, {"config": p})

        @pl.when(p == c)
        def _():
            keep(srs_src.at[q], srs_buf.at[c], srs_r)

        return carry

    lax.fori_loop(6, 16, send_sage, 0)
    lax.fori_loop(0, 6, send_sage, 0)

    through_weights(1, parts)
    hub_part = hub_first + mm(hub_t[:, 256:512], gacat[256:512, :])
    hg_src[...] = jnp.concatenate(
        [hub_part[:, :F].reshape(16, 8, F), hub_part[:, F:].reshape(16, 8, F)], axis=1
    ).astype(BF)

    def send_hub_grad(k, carry):
        s = lax.rem(g + k, n_g)
        send(hg_src.at[s], hg_buf.at[g], hg_s, hg_r, {"graph": s})
        return carry

    keep(hg_src.at[g], hg_buf.at[g], hg_r)
    lax.fori_loop(6, n_g, send_hub_grad, 0)
    lax.fori_loop(1, 6, send_hub_grad, 0)

    wait_bytes(ars_buf, ars_r)
    aag_src[...] = jnp.sum(ars_buf[...].astype(F32), axis=0).astype(BF)
    keep(aag_src, ga_h.at[c], aag_r)

    def send_attn_sum(k, carry):
        send(aag_src, ga_h.at[c], aag_s, aag_r, {"config": lax.rem(c + k, n_c)})
        return carry

    over_config(send_attn_sum)

    @pl.when(lax.rem(c, 2) == lax.rem(c // 4, 2))
    def _():
        wait_bytes(srs_buf, srs_r)
        sag_src[...] = jnp.sum(srs_buf[...].astype(F32), axis=0).astype(BF)
        keep(sag_src, gs_h.at[c // 2], sag_r)

        def send_sage_sum(k, carry):
            send(sag_src, gs_h.at[c // 2], sag_s, sag_r, {"config": lax.rem(c + k, n_c)})
            return carry

        over_config(send_sage_sum)

    def back_rows(b, carry):
        rows = pl.ds(pl.multiple_of(b * 128, 128), 128)
        nodes = pl.ds(b * 8, 8)
        tot32[nodes] = tot32[nodes] + mm(adj_t[rows, :], gacat[...]).reshape(8, 2, 8, 256)
        return carry

    lax.fori_loop(0, 4, back_rows, 0)

    lane_id = lax.broadcasted_iota(jnp.int32, (512, F), 1)
    node_id = lax.broadcasted_iota(jnp.int32, (512, F), 0)
    want_t = jnp.full((512, F), -1, jnp.int32)
    for j in range(8):
        want_t = jnp.where((lane_id == j) | (lane_id == j + 8), ids[j] - base, want_t)
    onehot_t = jnp.where(node_id == want_t, 1.0, 0.0).astype(BF)

    wait_bytes(hg_buf, hg_r)
    hub_sum = jnp.sum(hg_buf[...].astype(F32), axis=0)
    hub_both = jnp.concatenate([hub_sum[0:8], hub_sum[8:16]], axis=1)
    high = hub_both.astype(BF).astype(F32)
    hub_mat = jnp.concatenate([high, hub_both - high, jnp.zeros((112, 256), F32)], axis=0).astype(BF)
    total = (tot32[...].reshape(512, 256) + mm(onehot_t, hub_mat)).astype(BF)
    gf_out[0] = total[:, :F]
    gf_out[1] = total[:, F:]
    store_gf = pltpu.make_async_copy(gf_out, gf_h, out_sem.at[1])
    store_gf.start()

    wait_bytes(ga_h, aag_r)
    wait_bytes(gs_h, sag_r)

    wait_bytes(hub_all.at[pl.ds(0, 15)], hub_s)
    for h in range(2):
        wait_bytes(hall.at[h, pl.ds(0, 31)], fwd_s.at[h])
        wait_bytes(gback.at[h, pl.ds(0, 31)], back_s.at[h])
    wait_bytes(ars_buf.at[pl.ds(0, 31)], ars_s)
    wait_bytes(hg_buf.at[pl.ds(0, 15)], hg_s)
    wait_bytes(ars_buf.at[pl.ds(0, 31)], aag_s)

    @pl.when(lax.rem(c, 2) == lax.rem(c // 4, 2))
    def _():
        wait_bytes(srs_buf.at[pl.ds(0, 15)], srs_s)
        wait_bytes(ars_buf.at[pl.ds(0, 31)], sag_s)

    @pl.when(lax.rem(c, 2) != lax.rem(c // 4, 2))
    def _():
        wait_bytes(srs_buf.at[pl.ds(0, 16)], srs_s)

    store_lo.wait()
    store_gf.wait()


def finish(lo_h, gf_h, ga_h, gs_h, lo_out, gf_out, gw_out, lo, gf, ga, gs, gw, in_sem, out_sem):
    loads = [pltpu.make_async_copy(ga_h, ga, in_sem.at[0]), pltpu.make_async_copy(gs_h, gs, in_sem.at[1])]
    stores = [pltpu.make_async_copy(gw.at[0, i], gw_out.at[0, i], out_sem.at[i]) for i in range(6)]
    for a_h, a, a_out, size in ((lo_h, lo, lo_out, 16), (gf_h, gf, gf_out, 1)):
        for i in range(a.shape[0] // size):
            part = pl.ds(i * size, size)
            loads.append(pltpu.make_async_copy(a_h.at[part], a.at[part], in_sem.at[len(loads)]))
            stores.append(pltpu.make_async_copy(a.at[part], a_out.at[part], out_sem.at[len(stores)]))
    for load in loads:
        load.start()
    scale = 1.0 / math.sqrt(64 * 512)
    loads[0].wait()
    for i in range(4):
        gw[0, 2 + i] = ga[i * 8 : (i + 1) * 8].astype(F32).reshape(F, F) * scale
        stores[2 + i].start()
    loads[1].wait()
    for i in range(2):
        gw[0, i] = gs[i * 8 : (i + 1) * 8].astype(F32).reshape(F, F) * scale
        stores[i].start()
    for load, store in zip(loads[2:], stores[6:]):
        load.wait()
        store.start()
    for store in stores:
        store.wait()


def local(features, cotangent, sage_weight, attn_weight, tile_vals, tile_dst, tile_src, tile_count, hub_ids, hub_weight):
    hbm = pl.BlockSpec(memory_space=pltpu.HBM)
    v = pltpu.VMEM
    made = pl.pallas_call(
        kernel,
        out_shape=(
            jax.ShapeDtypeStruct((64, 16, F), BF),
            jax.ShapeDtypeStruct((2, 512, F), BF),
            jax.ShapeDtypeStruct((32, 16, F), BF),
            jax.ShapeDtypeStruct((16, 16, F), BF),
        ),
        in_specs=[hbm] * 10,
        out_specs=(hbm,) * 4,
        scratch_shapes=[
            v((2, 512, F), BF),
            v((64, 16, F), BF),
            v((2, F, F), BF),
            v((4, F, F), BF),
            v((12, F, F), BF),
            v((512, F), BF),
            pltpu.SMEM((12,), jnp.int32),
            pltpu.SMEM((12,), jnp.int32),
            pltpu.SMEM((1,), jnp.int32),
            pltpu.SMEM((8,), jnp.int32),
            v((64, 16, F), BF),
            v((2, 512, F), BF),
            v((512, 512), BF),
            v((512, 512), BF),
            v((128, 512), BF),
            v((256, 1024), BF),
            v((512, 256), F32),
            v((1024, F), F32),
            v((2, 512, F), BF),
            v((2, 32, 16, F), BF),
            v((2, 32, 16, F), BF),
            v((1024, F), F32),
            v((1024, F), F32),
            v((1024, F), F32),
            v((1024, F), F32),
            v((1024, 384), BF),
            v((1024, F), BF),
            v((1024, F), BF),
            v((1024, F), BF),
            v((1024, F), BF),
            v((2, 32, 16, F), BF),
            v((2, 32, 16, F), BF),
            v((1024, F), BF),
            v((512, 256), BF),
            v((32, 2, 8, 256), F32),
            v((16, F), BF),
            v((16, 16, F), BF),
            v((16, 16, F), BF),
            v((16, 16, F), BF),
            v((32, 16, F), BF),
            v((32, 16, F), BF),
            v((16, F), BF),
            v((16, 16, F), BF),
            v((32, 16, F), BF),
            v((16, F), BF),
        ]
        + [pltpu.SemaphoreType.DMA((2,))] * 4
        + [pltpu.SemaphoreType.DMA] * 12
        + [pltpu.SemaphoreType.DMA((10,)), pltpu.SemaphoreType.DMA((2,))],
        compiler_params=pltpu.CompilerParams(
            collective_id=0, has_side_effects=True, vmem_limit_bytes=60 * 2**20
        ),
    )(features, cotangent, sage_weight, attn_weight, tile_vals, tile_dst, tile_src, tile_count, hub_ids, hub_weight)
    return pl.pallas_call(
        finish,
        out_shape=(
            jax.ShapeDtypeStruct((64, 16, F), BF),
            jax.ShapeDtypeStruct((2, 512, F), BF),
            jax.ShapeDtypeStruct((1, 6, F, F), F32),
        ),
        in_specs=[hbm] * 4,
        out_specs=(hbm,) * 3,
        scratch_shapes=[
            v((64, 16, F), BF),
            v((2, 512, F), BF),
            v((32, 16, F), BF),
            v((16, 16, F), BF),
            v((1, 6, F, F), F32),
            pltpu.SemaphoreType.DMA((8,)),
            pltpu.SemaphoreType.DMA((12,)),
        ],
        compiler_params=pltpu.CompilerParams(vmem_limit_bytes=60 * 2**20),
    )(*made)


def solution(mesh):
    return jax.shard_map(
        local,
        mesh=mesh,
        in_specs=(
            P("config", "graph", None),
            P(None, ("graph", "config"), None),
            P(),
            P(),
            P("graph", None, None),
            P("graph"),
            P("graph"),
            P("graph"),
            P("graph"),
            P("graph", None),
        ),
        out_specs=(
            P(None, ("graph", "config"), None),
            P("config", "graph", None),
            P("graph", None, None, None),
        ),
        check_vma=False,
    )
```

```python
import functools
import math

import jax
import jax.numpy as jnp
from jax import lax
from jax.experimental import pallas as pl
from jax.experimental.pallas import tpu as pltpu
from jax.sharding import PartitionSpec as P

HEADS = 4
CAP = 20.0
F = 128
MESH = pl.DeviceIdType.MESH
BF = jnp.bfloat16
F32 = jnp.float32


def mm(a, b):
    return jnp.dot(a, b, preferred_element_type=F32)


def mm_nt(a, b):
    return lax.dot_general(a, b, (((1,), (1,)), ((), ())), preferred_element_type=F32)


def mm_tn(a, b):
    return lax.dot_general(a, b, (((0,), (0,)), ((), ())), preferred_element_type=F32)


def kernel(
    feat_h, cot_h, sw_h, aw_h, tiles_h, dst_h, src_h, cnt_h, ids_h, hubw_h,
    lo_h, gf_h, ga_h, gs_h,
    feat, cot, sw, aw, tiles, hubw, dst, src, cnt, ids, lo_out, gf_out,
    adj, adj_t, hub_t, fa_t, acc32, dsil, agg, hsend, hall, h32, c32, g32, o32,
    dqkv, hn, mixn, cotn, gmn, gsend, gback, gacat, tot32,
    hubloc, hub_all, hg_src, hg_buf, ars_src, ars_buf, aag_src,
    srs_src, srs_buf, sag_src,
    fwd_s, fwd_r, back_s, back_r, hub_s, hub_r, hg_s, hg_r,
    ars_s, ars_r, aag_s, aag_r, srs_s, srs_r, sag_s, sag_r, in_sem, out_sem,
):
    g = lax.axis_index("graph")
    c = lax.axis_index("config")
    n_g = lax.axis_size("graph")
    n_c = lax.axis_size("config")
    barrier = pltpu.get_barrier_semaphore()

    def hello_config(k, carry):
        pl.semaphore_signal(barrier, inc=1, device_id={"config": lax.rem(c + k, n_c)}, device_id_type=MESH)
        return carry

    def hello_graph(k, carry):
        pl.semaphore_signal(barrier, inc=1, device_id={"graph": lax.rem(g + k, n_g)}, device_id_type=MESH)
        return carry

    def over_config(one):
        lax.fori_loop(12, n_c, one, 0)
        lax.fori_loop(1, 12, one, 0)

    over_config(hello_config)
    lax.fori_loop(1, n_g, hello_graph, 0)
    loads = [
        pltpu.make_async_copy(a, b, in_sem.at[i])
        for i, (a, b) in enumerate(
            (
                (feat_h, feat), (ids_h, ids), (tiles_h, tiles), (dst_h, dst), (src_h, src),
                (cnt_h, cnt), (hubw_h, hubw), (sw_h, sw), (cot_h, cot), (aw_h, aw),
            )
        )
    ]
    for load in loads:
        load.start()

    def send(src_ref, dst_ref, send_sem, recv_sem, where):
        pltpu.make_async_remote_copy(
            src_ref=src_ref, dst_ref=dst_ref, send_sem=send_sem, recv_sem=recv_sem,
            device_id=where, device_id_type=MESH,
        ).start()

    def keep(src_ref, dst_ref, sem):
        pltpu.make_async_copy(src_ref, dst_ref, sem).start()

    def wait_bytes(ref, sem):
        pltpu.make_async_copy(ref, ref, sem).wait()

    loads[0].wait()
    loads[1].wait()
    base = g * 512
    row = lax.broadcasted_iota(jnp.int32, (16, 512), 0)
    col = lax.broadcasted_iota(jnp.int32, (16, 512), 1)
    want = jnp.full((16, 512), -1, jnp.int32)
    for j in range(8):
        want = jnp.where(row == j, ids[j] - base, want)
    onehot = jnp.where(col == want, 1.0, 0.0).astype(BF)
    x_cat = jnp.concatenate([feat[0], feat[1]], axis=1)
    rows_hub = mm(onehot, x_cat)
    hubloc[...] = jnp.concatenate([rows_hub[:8, :F], rows_hub[:8, F:]], axis=0).astype(BF)

    pl.semaphore_wait(barrier, n_g + n_c - 2)

    keep(hubloc, hub_all.at[g], hub_r)

    def send_hub(k, carry):
        send(hubloc, hub_all.at[g], hub_s, hub_r, {"graph": lax.rem(g + k, n_g)})
        return carry

    lax.fori_loop(6, n_g, send_hub, 0)
    lax.fori_loop(1, 6, send_hub, 0)

    for load in loads[2:]:
        load.wait()

    def halves(block):
        groups = block.shape[0] // 16
        split = block.reshape(groups, 2, 8, block.shape[1])
        return [split[:, h].reshape(groups * 8, block.shape[1]) for h in range(2)]

    def build(pair, carry):
        for s in range(4):
            found = []
            for b_in in range(2):
                b = pair * 2 + b_in
                acc = jnp.zeros((128, 128), F32)
                for t in range(12):
                    live = (dst[t] == b) & (src[t] == s) & (t < cnt[0])
                    acc = acc + jnp.where(live, 1.0, 0.0) * tiles[t].astype(F32)
                adj[pl.ds(pl.multiple_of(b * 128, 128), 128), s * 128 : (s + 1) * 128] = acc.astype(BF)
                found.append(acc)
            split = halves(jnp.concatenate(found, axis=0))
            for h in range(2):
                columns = pl.ds(pl.multiple_of(h * 256 + pair * 128, 128), 128)
                adj_t[s * 128 : (s + 1) * 128, columns] = split[h].T.astype(BF)
        return carry

    lax.fori_loop(0, 2, build, 0)

    def first(b, carry):
        rows = pl.ds(pl.multiple_of(b * 128, 128), 128)
        acc32[rows, :] = mm(adj[rows, :], jnp.concatenate([feat[0], feat[1]], axis=1))
        return carry

    lax.fori_loop(0, 4, first, 0)

    wait_bytes(hub_all, hub_r)
    hubs = hub_all[...].astype(F32).reshape(16, 2, 8, F)
    hub_cat = jnp.concatenate(
        [hubs[:, 0].reshape(128, F).astype(BF), hubs[:, 1].reshape(128, F).astype(BF)], axis=1
    )
    w_sage = sw[...].reshape(2 * F, F)

    def to_half(h):
        def one(k, carry):
            p = lax.rem(c + k, n_c)
            send(hsend.at[h, p], hall.at[h, c], fwd_s.at[h], fwd_r.at[h], {"config": p})
            return carry

        return one

    def forward(i, carry):
        b = lax.rem(c // 8 + 2 + i, 4)
        rows = pl.ds(pl.multiple_of(b * 128, 128), 128)
        acc = acc32[rows, :] + mm(hubw[rows, :], hub_cat)
        hidden, slope = [], []
        for l in range(2):
            a_l = acc[:, l * F : (l + 1) * F].astype(BF)
            agg[l, rows, :] = a_l
            pre = mm(jnp.concatenate([feat[l, rows, :], a_l], axis=1), w_sage)
            sig = 0.5 + 0.5 * jnp.tanh(0.5 * pre)
            slope.append(halves(sig * (1.0 + pre * (1.0 - sig))))
            hidden.append(halves(pre * sig))
        for h in range(2):
            for l in range(2):
                dsil[pl.ds(pl.multiple_of((h * 2 + l) * 256 + b * 64, 64), 64), :] = slope[l][h]
            hsend[h, pl.ds(b * 8, 8)] = jnp.concatenate(
                [hidden[0][h].reshape(8, 8, F), hidden[1][h].reshape(8, 8, F)], axis=1
            ).astype(BF)

        def send_hidden(k, inner):
            p = b * 8 + lax.rem(c + k, 8)

            @pl.when(p != c)
            def _():
                send(hsend.at[0, p], hall.at[0, c], fwd_s.at[0], fwd_r.at[0], {"config": p})

            return inner

        lax.fori_loop(0, 8, send_hidden, 0)
        return carry

    lax.fori_loop(0, 4, forward, 0)
    over_config(to_half(1))
    for h in range(2):
        keep(hsend.at[h, c], hall.at[h, c], fwd_r.at[h])

    c32[...] = cot[...].astype(F32).reshape(1024, F)

    def cot_nodes(i, carry):
        rows = pl.ds(pl.multiple_of(i * 256, 256), 256)
        part = jnp.concatenate(
            [c32[pl.ds(i * 4 + k, 64, stride=16), :] for k in range(4)], axis=0
        ).astype(BF)
        cotn[rows, :] = part
        gmn[rows, :] = mm_nt(part, aw[3]).astype(BF)
        return carry

    lax.fori_loop(0, 4, cot_nodes, 0)

    split_hub = halves(hubw[...].astype(F32))
    for h in range(2):
        hub_t[:, h * 256 : (h + 1) * 256] = split_hub[h].T.astype(BF)
    for l in range(2):
        split_feat = halves(feat[l].astype(F32))
        split_agg = halves(agg[l].astype(F32))
        for h in range(2):
            columns = slice((h * 2 + l) * 256, (h * 2 + l + 1) * 256)
            fa_t[0:F, columns] = split_feat[h].T.astype(BF)
            fa_t[F : 2 * F, columns] = split_agg[h].T.astype(BF)

    w_qkv = jnp.concatenate([aw[0], aw[1], aw[2]], axis=1)

    def head_of(shape, dim, width):
        return lax.broadcasted_iota(jnp.int32, shape, dim) // width

    head_mask = jnp.where(
        head_of((256, F), 0, 64) == head_of((256, F), 1, 32), 1.0, 0.0
    ).astype(BF)
    zeros = jnp.zeros((64, F), BF)
    lane = lax.broadcasted_iota(jnp.int32, (64, F), 1)

    def own_head(full):
        return jnp.where(
            lane < 64,
            jnp.where(lane < 32, full[0:64], full[64:128]),
            jnp.where(lane < 96, full[128:192], full[192:256]),
        )

    root = 1.0 / math.sqrt(32.0)

    def attend(i, carry):
        rows = pl.ds(pl.multiple_of(i * 256, 256), 256)
        start = (i // 2) * 512 + lax.rem(i, 2) * 4
        h_b = jnp.concatenate([h32[pl.ds(start + k, 64, stride=8), :] for k in range(4)], axis=0).astype(BF)
        hn[rows, :] = h_b
        qkv = mm(h_b, w_qkv).astype(BF)
        four = range(4)
        q = [qkv[k * 64 : (k + 1) * 64, 0:F] for k in four]
        key_x = [jnp.concatenate([qkv[k * 64 : (k + 1) * 64, F : 2 * F]] * 4, axis=0) * head_mask for k in four]
        val_x = [
            jnp.concatenate(
                [jnp.concatenate([qkv[k * 64 : (k + 1) * 64, 2 * F : 3 * F]] * 4, axis=0) * head_mask, head_mask],
                axis=1,
            )
            for k in four
        ]
        t = [jnp.tanh(mm_nt(q[k], key_x[k]) * (root / CAP)) for k in four]
        w = [jnp.exp(CAP * t[k]).astype(BF) for k in four]
        both = [mm(w[k], val_x[k]) for k in four]
        inv = [1.0 / both[k][:, F:] for k in four]
        mix = [both[k][:, :F] * inv[k] for k in four]
        gm = [gmn[pl.ds(pl.multiple_of(i * 256 + k * 64, 64), 64), :].astype(F32) * inv[k] for k in four]
        gm_b = [gm[k].astype(BF) for k in four]
        less = jnp.concatenate([(gm_b[k].astype(F32) * mix[k]).astype(BF) for k in four], axis=0)
        less = mm_nt(less, head_mask)
        dp = [mm_nt(gm_b[k], val_x[k][:, :F]) - less[k * 64 : (k + 1) * 64] for k in four]
        ds = [(w[k].astype(F32) * dp[k] * ((1.0 - t[k] * t[k]) * root)).astype(BF) for k in four]
        d_q = [mm(ds[k], key_x[k]).astype(BF) for k in four]
        right = [
            jnp.concatenate(
                [jnp.concatenate([q[k], zeros], axis=1), jnp.concatenate([zeros, gm_b[k]], axis=1)], axis=0
            )
            for k in four
        ]
        d_kv = [mm_tn(jnp.concatenate([ds[k], w[k]], axis=0), right[k]) for k in four]
        d_k = [own_head(d_kv[k][:, :F]).astype(BF) for k in four]
        d_v = [own_head(d_kv[k][:, F:]).astype(BF) for k in four]
        mixes = [mix[k].astype(BF) for k in four]
        mix_b = jnp.concatenate(mixes, axis=0)
        mixn[rows, :] = mix_b
        grads = jnp.concatenate(
            [jnp.concatenate(d_q, axis=0), jnp.concatenate(d_k, axis=0), jnp.concatenate(d_v, axis=0)],
            axis=1,
        )
        dqkv[rows, :] = grads
        back = cotn[rows, :].astype(F32) + mm_nt(grads, w_qkv)
        for k in range(4):
            g32[pl.ds(start + k, 64, stride=8), :] = back[k * 64 : (k + 1) * 64]
        return carry

    def half_of_nodes(h, carry):
        rows = pl.ds(pl.multiple_of(h * 512, 512), 512)
        wait_bytes(hall.at[h], fwd_r.at[h])
        h32[rows, :] = hall[h].astype(F32).reshape(512, F)
        lax.fori_loop(0, 2, lambda j, x: attend(h * 2 + j, x), 0, unroll=True)
        gsend[h] = g32[rows, :].reshape(32, 16, F).astype(BF)

        def send_back(k, inner):
            p = lax.rem(c + k, n_c)
            send(gsend.at[h, p], gback.at[h, c], back_s.at[h], back_r.at[h], {"config": p})
            return inner

        over_config(send_back)
        keep(gsend.at[h, c], gback.at[h, c], back_r.at[h])
        return carry

    lax.fori_loop(0, 2, half_of_nodes, 0)

    def outputs(i, carry):
        rows = pl.ds(pl.multiple_of(i * 256, 256), 256)
        out = hn[rows, :].astype(F32) + mm(mixn[rows, :], aw[3])
        for k in range(4):
            o32[pl.ds(i * 4 + k, 64, stride=16), :] = out[k * 64 : (k + 1) * 64]
        return carry

    lax.fori_loop(0, 4, outputs, 0)
    lo_out[...] = o32[...].reshape(64, 16, F).astype(BF)
    store_lo = pltpu.make_async_copy(lo_out, lo_h, out_sem.at[0])
    store_lo.start()
    part_qkv = mm_tn(hn[...], dqkv[...])
    part_o = mm_tn(mixn[...], cotn[...])
    for i in range(3):
        ars_src[i * 8 : (i + 1) * 8] = part_qkv[:, i * F : (i + 1) * F].reshape(8, 16, F).astype(BF)
    ars_src[24:32] = part_o.reshape(8, 16, F).astype(BF)

    def send_attn(k, carry):
        p = lax.rem(c + k, n_c)
        send(ars_src.at[p], ars_buf.at[c], ars_s, ars_r, {"config": p})
        return carry


    def slopes(h):
        wait_bytes(gback.at[h], back_r.at[h])
        arrived = gback[h].astype(F32).reshape(32, 2, 8, F)
        parts = []
        for l in range(2):
            rows = slice((h * 2 + l) * 256, (h * 2 + l + 1) * 256)
            parts.append((arrived[:, l].reshape(256, F) * dsil[rows, :]).astype(BF))
        return parts

    def through_weights(h, parts):
        for l in range(2):
            both = mm_nt(parts[l], w_sage)
            tot32[:, h, :, l * F : (l + 1) * F] = both[:, :F].reshape(32, 8, F)
            gacat[h * 256 : (h + 1) * 256, l * F : (l + 1) * F] = both[:, F:].astype(BF)

    parts = slopes(0)
    through_weights(0, parts)
    sage_first = mm(fa_t[:, 0:256], parts[0]) + mm(fa_t[:, 256:512], parts[1])
    hub_first = mm(hub_t[:, 0:256], gacat[0:256, :])
    keep(ars_src.at[c], ars_buf.at[c], ars_r)
    over_config(send_attn)
    parts = slopes(1)
    sage_all = sage_first + mm(fa_t[:, 512:768], parts[0]) + mm(fa_t[:, 768:1024], parts[1])
    srs_src[...] = sage_all.reshape(16, 16, F).astype(BF)

    def send_sage(k, carry):
        q = lax.rem(c // 2 + k, 16)
        p = q * 2 + lax.rem(q // 2, 2)

        @pl.when(p != c)
        def _():
            send(srs_src.at[q], srs_buf.at[c], srs_s, srs_r, {"config": p})

        @pl.when(p == c)
        def _():
            keep(srs_src.at[q], srs_buf.at[c], srs_r)

        return carry

    lax.fori_loop(6, 16, send_sage, 0)
    lax.fori_loop(0, 6, send_sage, 0)

    through_weights(1, parts)
    hub_part = hub_first + mm(hub_t[:, 256:512], gacat[256:512, :])
    hg_src[...] = jnp.concatenate(
        [hub_part[:, :F].reshape(16, 8, F), hub_part[:, F:].reshape(16, 8, F)], axis=1
    ).astype(BF)

    def send_hub_grad(k, carry):
        s = lax.rem(g + k, n_g)
        send(hg_src.at[s], hg_buf.at[g], hg_s, hg_r, {"graph": s})
        return carry

    keep(hg_src.at[g], hg_buf.at[g], hg_r)
    lax.fori_loop(6, n_g, send_hub_grad, 0)
    lax.fori_loop(1, 6, send_hub_grad, 0)

    wait_bytes(ars_buf, ars_r)
    aag_src[...] = jnp.sum(ars_buf[...].astype(F32), axis=0).astype(BF)
    keep(aag_src, ga_h.at[c], aag_r)

    def send_attn_sum(k, carry):
        send(aag_src, ga_h.at[c], aag_s, aag_r, {"config": lax.rem(c + k, n_c)})
        return carry

    over_config(send_attn_sum)

    @pl.when(lax.rem(c, 2) == lax.rem(c // 4, 2))
    def _():
        wait_bytes(srs_buf, srs_r)
        sag_src[...] = jnp.sum(srs_buf[...].astype(F32), axis=0).astype(BF)
        keep(sag_src, gs_h.at[c // 2], sag_r)

        def send_sage_sum(k, carry):
            send(sag_src, gs_h.at[c // 2], sag_s, sag_r, {"config": lax.rem(c + k, n_c)})
            return carry

        over_config(send_sage_sum)

    def back_rows(b, carry):
        rows = pl.ds(pl.multiple_of(b * 128, 128), 128)
        nodes = pl.ds(b * 8, 8)
        tot32[nodes] = tot32[nodes] + mm(adj_t[rows, :], gacat[...]).reshape(8, 2, 8, 256)
        return carry

    lax.fori_loop(0, 4, back_rows, 0)

    lane_id = lax.broadcasted_iota(jnp.int32, (512, F), 1)
    node_id = lax.broadcasted_iota(jnp.int32, (512, F), 0)
    want_t = jnp.full((512, F), -1, jnp.int32)
    for j in range(8):
        want_t = jnp.where((lane_id == j) | (lane_id == j + 8), ids[j] - base, want_t)
    onehot_t = jnp.where(node_id == want_t, 1.0, 0.0).astype(BF)

    wait_bytes(hg_buf, hg_r)
    hub_sum = jnp.sum(hg_buf[...].astype(F32), axis=0)
    hub_both = jnp.concatenate([hub_sum[0:8], hub_sum[8:16]], axis=1)
    high = hub_both.astype(BF).astype(F32)
    hub_mat = jnp.concatenate([high, hub_both - high, jnp.zeros((112, 256), F32)], axis=0).astype(BF)
    total = (tot32[...].reshape(512, 256) + mm(onehot_t, hub_mat)).astype(BF)
    gf_out[0] = total[:, :F]
    gf_out[1] = total[:, F:]
    store_gf = pltpu.make_async_copy(gf_out, gf_h, out_sem.at[1])
    store_gf.start()

    wait_bytes(ga_h, aag_r)
    wait_bytes(gs_h, sag_r)

    wait_bytes(hub_all.at[pl.ds(0, 15)], hub_s)
    for h in range(2):
        wait_bytes(hall.at[h, pl.ds(0, 31)], fwd_s.at[h])
        wait_bytes(gback.at[h, pl.ds(0, 31)], back_s.at[h])
    wait_bytes(ars_buf.at[pl.ds(0, 31)], ars_s)
    wait_bytes(hg_buf.at[pl.ds(0, 15)], hg_s)
    wait_bytes(ars_buf.at[pl.ds(0, 31)], aag_s)

    @pl.when(lax.rem(c, 2) == lax.rem(c // 4, 2))
    def _():
        wait_bytes(srs_buf.at[pl.ds(0, 15)], srs_s)
        wait_bytes(ars_buf.at[pl.ds(0, 31)], sag_s)

    @pl.when(lax.rem(c, 2) != lax.rem(c // 4, 2))
    def _():
        wait_bytes(srs_buf.at[pl.ds(0, 16)], srs_s)

    store_lo.wait()
    store_gf.wait()


def finish(lo_h, gf_h, ga_h, gs_h, lo_out, gf_out, gw_out, lo, gf, ga, gs, gw, in_sem, out_sem):
    loads = [pltpu.make_async_copy(ga_h, ga, in_sem.at[0]), pltpu.make_async_copy(gs_h, gs, in_sem.at[1])]
    stores = [pltpu.make_async_copy(gw.at[0, i], gw_out.at[0, i], out_sem.at[i]) for i in range(6)]
    for a_h, a, a_out, size in ((lo_h, lo, lo_out, 16), (gf_h, gf, gf_out, 1)):
        for i in range(a.shape[0] // size):
            part = pl.ds(i * size, size)
            loads.append(pltpu.make_async_copy(a_h.at[part], a.at[part], in_sem.at[len(loads)]))
            stores.append(pltpu.make_async_copy(a.at[part], a_out.at[part], out_sem.at[len(stores)]))
    for load in loads:
        load.start()
    scale = 1.0 / math.sqrt(64 * 512)
    loads[0].wait()
    for i in range(4):
        gw[0, 2 + i] = ga[i * 8 : (i + 1) * 8].astype(F32).reshape(F, F) * scale
        stores[2 + i].start()
    loads[1].wait()
    for i in range(2):
        gw[0, i] = gs[i * 8 : (i + 1) * 8].astype(F32).reshape(F, F) * scale
        stores[i].start()
    for load, store in zip(loads[2:], stores[6:]):
        load.wait()
        store.start()
    for store in stores:
        store.wait()


def local(features, cotangent, sage_weight, attn_weight, tile_vals, tile_dst, tile_src, tile_count, hub_ids, hub_weight):
    hbm = pl.BlockSpec(memory_space=pltpu.HBM)
    v = pltpu.VMEM
    made = pl.pallas_call(
        kernel,
        out_shape=(
            jax.ShapeDtypeStruct((64, 16, F), BF),
            jax.ShapeDtypeStruct((2, 512, F), BF),
            jax.ShapeDtypeStruct((32, 16, F), BF),
            jax.ShapeDtypeStruct((16, 16, F), BF),
        ),
        in_specs=[hbm] * 10,
        out_specs=(hbm,) * 4,
        scratch_shapes=[
            v((2, 512, F), BF),
            v((64, 16, F), BF),
            v((2, F, F), BF),
            v((4, F, F), BF),
            v((12, F, F), BF),
            v((512, F), BF),
            pltpu.SMEM((12,), jnp.int32),
            pltpu.SMEM((12,), jnp.int32),
            pltpu.SMEM((1,), jnp.int32),
            pltpu.SMEM((8,), jnp.int32),
            v((64, 16, F), BF),
            v((2, 512, F), BF),
            v((512, 512), BF),
            v((512, 512), BF),
            v((128, 512), BF),
            v((256, 1024), BF),
            v((512, 256), F32),
            v((1024, F), F32),
            v((2, 512, F), BF),
            v((2, 32, 16, F), BF),
            v((2, 32, 16, F), BF),
            v((1024, F), F32),
            v((1024, F), F32),
            v((1024, F), F32),
            v((1024, F), F32),
            v((1024, 384), BF),
            v((1024, F), BF),
            v((1024, F), BF),
            v((1024, F), BF),
            v((1024, F), BF),
            v((2, 32, 16, F), BF),
            v((2, 32, 16, F), BF),
            v((512, 256), BF),
            v((32, 2, 8, 256), F32),
            v((16, F), BF),
            v((16, 16, F), BF),
            v((16, 16, F), BF),
            v((16, 16, F), BF),
            v((32, 16, F), BF),
            v((32, 16, F), BF),
            v((16, F), BF),
            v((16, 16, F), BF),
            v((32, 16, F), BF),
            v((16, F), BF),
        ]
        + [pltpu.SemaphoreType.DMA((2,))] * 4
        + [pltpu.SemaphoreType.DMA] * 12
        + [pltpu.SemaphoreType.DMA((10,)), pltpu.SemaphoreType.DMA((2,))],
        compiler_params=pltpu.CompilerParams(
            collective_id=0, has_side_effects=True, vmem_limit_bytes=60 * 2**20
        ),
    )(features, cotangent, sage_weight, attn_weight, tile_vals, tile_dst, tile_src, tile_count, hub_ids, hub_weight)
    return pl.pallas_call(
        finish,
        out_shape=(
            jax.ShapeDtypeStruct((64, 16, F), BF),
            jax.ShapeDtypeStruct((2, 512, F), BF),
            jax.ShapeDtypeStruct((1, 6, F, F), F32),
        ),
        in_specs=[hbm] * 4,
        out_specs=(hbm,) * 3,
        scratch_shapes=[
            v((64, 16, F), BF),
            v((2, 512, F), BF),
            v((32, 16, F), BF),
            v((16, 16, F), BF),
            v((1, 6, F, F), F32),
            pltpu.SemaphoreType.DMA((8,)),
            pltpu.SemaphoreType.DMA((12,)),
        ],
        compiler_params=pltpu.CompilerParams(vmem_limit_bytes=60 * 2**20),
    )(*made)


def solution(mesh):
    return jax.shard_map(
        local,
        mesh=mesh,
        in_specs=(
            P("config", "graph", None),
            P(None, ("graph", "config"), None),
            P(),
            P(),
            P("graph", None, None),
            P("graph"),
            P("graph"),
            P("graph"),
            P("graph"),
            P("graph", None),
        ),
        out_specs=(
            P(None, ("graph", "config"), None),
            P("config", "graph", None),
            P("graph", None, None, None),
        ),
        check_vma=False,
    )
```
